512 devices in a mesh: blk: 8 (over z_lo), tok: 64 (over z_hi, x, y, core).
Axes of the slice: x: 4, y: 4, z: 16 (z_hi: 2, z_lo: 8; z = z_hi * 8 + z_lo), core: 2. Of those that a mesh axis runs over, the one named last changes fastest.
Arguments:
- tokens: bfloat16 [16384, 8192], P('tok', 'blk'), may hold values from -6 to 6
- first_blocks: bfloat16 [64, 128, 128], P('blk'), may hold values from -0.5 to 0.5
- latter_factor_blocks: bfloat16 [64, 128, 128], P('blk'), may hold values from -0.5 to 0.5
- block_perm: int32 [64], replicated, may hold values from 0 to 63, each once
- out_grad: bfloat16 [16384, 8192], P('tok', 'blk'), may hold values from -6 to 6
Outputs:
- first_grad: float32 [64, 128, 128], P('blk', 'tok')
- latter_factor_gradient: float32 [64, 128, 128], P('blk', 'tok')
- input_grad: bfloat16 [16384, 8192], P('tok', 'blk')
The draws below stay inside these ranges and needn't reach their ends.
Inputs may be any that keep to these rules, and one draw needn't show every extreme that they name: block_perm holds each of 0 to 63 once.
All inputs are finite; a program needn't handle non-finite values.
Results may differ from the reference program's by a relative error of at most 0.0057.
Values may be sent and summed in bfloat16 or wider, within the bound.
A program may use at most 64 MiB of HBM per device.

```python
import jax
import jax.numpy as jnp
from jax import lax

NB = 64
BS = 128
TOK_DEV = 256
R = 2
D = 8192
TOKENS = 16384
N_TOK = 64


def block_scale(own_key, shape, shards, smallest, high):
    gain, own = 1.0, jax.random.fold_in(own_key, 6)
    for axis_at, parts in shards:
        steps = jnp.exp(jax.random.uniform(jax.random.fold_in(own, axis_at), (parts,), jnp.float32, smallest / len(shards), high / len(shards)))
        gain = gain * jnp.repeat(steps, shape[axis_at] // parts).reshape([-1 if axis == axis_at else 1 for axis in range(len(shape))])
    return gain


def normal_values(own_key, shape, width, limit, pieces=(), held_as=jnp.bfloat16):
    level = block_scale(own_key, shape, pieces, -0.22, 0.18) if pieces else 1.0
    result = jax.random.normal(own_key, shape, jnp.float32) * width * level
    return jnp.minimum(jnp.maximum(result, -limit), limit).astype(held_as)


def setup_inputs(seed: int = 0) -> dict:
    seeds = jax.random.split(jax.random.key(seed), 6)
    tokens = normal_values(seeds[0], (TOKENS, D), 1.0, 6.0, ((0, 64), (1, 8)))
    first_blocks = normal_values(seeds[1], (NB, BS, BS), BS ** -0.5, 0.5, ((0, 8),))
    latter_factor_blocks = normal_values(seeds[2], (NB, BS, BS), BS ** -0.5, 0.5, ((0, 8),))
    block_perm = jax.random.permutation(seeds[3], NB).astype(jnp.int32)
    out_grad = normal_values(seeds[4], (TOKENS, D), 1.0, 6.0, ((0, 64), (1, 8)))
    return dict(tokens=tokens, first_blocks=first_blocks, latter_factor_blocks=latter_factor_blocks, block_perm=block_perm, out_grad=out_grad)


def gelu_value(v):
    return 0.5 * v * (1.0 + lax.erf(v * 0.7071067811865476))


def gelu_derivative(v):
    return 0.5 * (1.0 + lax.erf(v * 0.7071067811865476)) + v * 0.3989422804014327 * jnp.exp(-0.5 * v * v)


def reference(tokens, first_blocks, latter_factor_blocks, block_perm, out_grad):
    order = jnp.arange(NB, dtype=jnp.int32)
    inverse = jnp.sum(jnp.where(block_perm[:, None] == order[None, :], order[:, None], 0), axis=0).astype(jnp.int32)
    first_w = first_blocks.astype(jnp.float32)
    second_w = latter_factor_blocks.astype(jnp.float32)

    def step(carry, pair):
        token_rows, grad_rows = pair
        rows = token_rows.shape[0]
        inputs = token_rows.reshape(rows, NB, BS).astype(jnp.float32)
        pre = jnp.einsum('tbi,bio->tbo', inputs, first_w)
        act = gelu_value(pre).astype(jnp.bfloat16)
        mixed = act.reshape(rows, NB, NB, R)[:, :, inverse, :].transpose(0, 2, 1, 3).reshape(rows, NB, BS)
        incoming_gradient = grad_rows.reshape(rows, NB, BS).astype(jnp.float32)
        second_acc = carry[1] + jnp.einsum('tdi,tdo->dio', mixed.astype(jnp.float32), incoming_gradient)
        permuted_gradient = jnp.einsum('tdo,dio->tdi', incoming_gradient, second_w).astype(jnp.bfloat16)
        act_grad = permuted_gradient.reshape(rows, NB, NB, R)[:, block_perm, :, :].transpose(0, 2, 1, 3).reshape(rows, NB, BS)
        pre_grad = (act_grad.astype(jnp.float32) * gelu_derivative(pre)).astype(jnp.bfloat16)
        pre_f = pre_grad.astype(jnp.float32)
        first_acc = carry[0] + jnp.einsum('tbi,tbo->bio', inputs, pre_f)
        input_rows = jnp.einsum('tbo,bio->tbi', pre_f, first_w).astype(jnp.bfloat16).reshape(rows, NB * BS)
        return (first_acc, second_acc), input_rows

    zeros = jnp.zeros((NB, BS, BS), jnp.float32)
    token_blocks = tokens.reshape(N_TOK, TOK_DEV, NB * BS)
    grad_blocks = out_grad.reshape(N_TOK, TOK_DEV, NB * BS)
    (first_grad, latter_factor_gradient), input_blocks = lax.scan(step, (zeros, zeros), (token_blocks, grad_blocks))
    return first_grad, latter_factor_gradient, input_blocks.reshape(TOKENS, NB * BS)
```

```python
import jax
import jax.numpy as jnp
from jax import lax
from jax.experimental import pallas as pl
from jax.experimental.pallas import tpu as pltpu
from jax.sharding import PartitionSpec as P

MESH = pl.DeviceIdType.MESH
F32 = jnp.float32
BF16 = jnp.bfloat16
ROWS = 256
BS = 128
NBL = 8


def dot_nn(a, b):
    return lax.dot_general(a, b, (((1,), (0,)), ((), ())), preferred_element_type=F32)


def dot_nt(a, b):
    return lax.dot_general(a, b, (((1,), (1,)), ((), ())), preferred_element_type=F32)


def dot_tn(a, b):
    return lax.dot_general(a, b, (((0,), (0,)), ((), ())), preferred_element_type=F32)


def iota(dim):
    return lax.broadcasted_iota(jnp.int32, (BS, BS), dim)


def one_hot(hit):
    return jnp.where(hit, 1.0, 0.0).astype(BF16)


def kernel(
    x_ref, w_ref, l_ref, perm_ref, og_ref,
    fg_ref, lg_ref, ig_ref,
    wm, tmp, dgelu, send_mg, recv_mg, send_act, recv_act,
    g_all, r_core, s_core, r_y, s_y, r_x, s_x, r_z,
    a2a_send, a2a_recv, rs_send, rs_recv,
):
    b = lax.axis_index("blk")
    t = lax.axis_index("tok")
    zh, x, y, core = t // 32, (t // 8) % 4, (t // 2) % 4, t % 2
    half, place = b // 4, b % 4

    def ring(at, k):
        return (at + k) % 4

    core_peer = (b, t + 1 - 2 * core)
    zh_peer = (b, t + 32 - 64 * zh)

    def y_peer(k):
        return (b, t + (ring(y, k) - y) * 2)

    def x_peer(k):
        return (b, t + (ring(x, k) - x) * 8)

    far = [(1 - half) * 4 + ring(place, k) for k in range(4)]
    near = [half * 4 + ring(place, k) for k in range(1, 4)]
    others = far + near

    barrier = pltpu.get_barrier_semaphore()
    peers = [(s, t) for s in others] + [core_peer, zh_peer]
    peers += [y_peer(k) for k in range(1, 4)] + [x_peer(k) for k in range(1, 4)]
    for peer in peers:
        pl.semaphore_signal(barrier, inc=1, device_id=peer, device_id_type=MESH)

    row, col = iota(0), iota(1)
    swap = one_hot(col == ((row >> 1) & 7) * 16 + (row >> 4) * 2 + (row & 1))
    by_core = one_hot(
        col
        == ((row >> 3) & 1) * 64
        + ((row >> 1) & 3) * 16
        + ((row >> 4) & 3) * 4
        + (row >> 6) * 2
        + (row & 1)
    )

    def slab(s):
        return pl.ds(pl.multiple_of(s * 16, 16), 16)

    def a2a(phase, s, send, recv):
        return pltpu.make_async_remote_copy(
            src_ref=send.at[s],
            dst_ref=recv.at[:, slab(b), :],
            send_sem=a2a_send.at[phase, s],
            recv_sem=a2a_recv.at[phase, b],
            device_id=(s, t),
            device_id_type=MESH,
        )

    def landed(phase, s, send, recv):
        return pltpu.make_async_remote_copy(
            src_ref=send.at[s],
            dst_ref=recv.at[:, slab(s), :],
            send_sem=a2a_send.at[phase, s],
            recv_sem=a2a_recv.at[phase, s],
            device_id=(s, t),
            device_id_type=MESH,
        )

    def swapped(s):
        chunk = tmp[:, slab(s), :].reshape(BS, ROWS)
        return dot_nn(swap, chunk).astype(BF16).reshape(NBL, 16, ROWS)

    for d in range(NBL):
        cols = slice(d * BS, (d + 1) * BS)
        tmp[d] = dot_nt(l_ref[d], og_ref[:, cols]).astype(BF16)
    for at, s in enumerate(others):
        send_mg[s] = swapped(s)
        if at == 0:
            pl.semaphore_wait(barrier, len(peers))
        a2a(0, s, send_mg, recv_mg).start()
    recv_mg[:, slab(b), :] = swapped(b)

    perm = jnp.broadcast_to(perm_ref[...].astype(F32), (16, 64)).astype(BF16)
    pair = one_hot(iota(1)[:64] // 2 == iota(0)[:64])
    target = dot_nn(perm, pair)[:1] * 2.0 + (iota(1)[:1] % 2).astype(F32)
    placing = one_hot(iota(0).astype(F32) == target)
    for a in range(NBL):
        cols = slice(a * BS, (a + 1) * BS)
        wm[a] = dot_nt(placing, w_ref[a]).astype(BF16)
        pre = dot_nt(wm[a], x_ref[:, cols])
        cdf = 0.5 * (1.0 + lax.erf(pre * 0.7071067811865476))
        tmp[a] = (pre * cdf).astype(BF16)
        dgelu[a] = cdf + pre * 0.3989422804014327 * jnp.exp(-0.5 * pre * pre)
    for s in others:
        send_act[s] = swapped(s)
        a2a(1, s, send_act, recv_act).start()
    recv_act[:, slab(b), :] = swapped(b)

    def copy(g, at_src, at_dst, src, dst, peer):
        return pltpu.make_async_remote_copy(
            src_ref=src,
            dst_ref=dst,
            send_sem=rs_send.at[g, at_src],
            recv_sem=rs_recv.at[g, at_dst],
            device_id=peer,
            device_id_type=MESH,
        )

    def core_half(c):
        return pl.ds(pl.multiple_of(c * 64, 64), 64)

    def scatter_sum(g, out_ref):
        sends = []
        copies = copy(
            g, 0, 0, g_all.at[g, :, core_half(1 - core), :], r_core.at[g], core_peer
        )
        copies.start()
        copies.wait_recv()
        sends.append(copies)
        s_core[g] = (
            g_all[g, :, core_half(core), :].astype(F32) + r_core[g].astype(F32)
        ).astype(BF16)
        for k in range(1, 4):
            to = ring(y, k)
            c = copy(
                g, 1 + to, 1 + y, s_core.at[g, :, slab(to), :], r_y.at[g, y], y_peer(k)
            )
            c.start()
            sends.append(c)
        total = s_core[g, :, slab(y), :].astype(F32)
        for k in range(1, 4):
            at = ring(y, k)
            copy(
                g, 1 + at, 1 + at, s_core.at[g, :, slab(at), :], r_y.at[g, at], y_peer(k)
            ).wait_recv()
            total = total + r_y[g, at].astype(F32)
        s_y[g] = (
            dot_nn(swap, total.astype(BF16).reshape(BS, BS))
            .astype(BF16)
            .reshape(2, 4, 16, BS)
        )
        for k in range(1, 4):
            to = ring(x, k)
            c = copy(g, 5 + to, 5 + x, s_y.at[g, :, to], r_x.at[g, x], x_peer(k))
            c.start()
            sends.append(c)
        total = s_y[g, :, x].astype(F32)
        for k in range(1, 4):
            at = ring(x, k)
            copy(
                g, 5 + at, 5 + at, s_y.at[g, :, at], r_x.at[g, at], x_peer(k)
            ).wait_recv()
            total = total + r_x[g, at].astype(F32)
        s_x[g] = total
        c = copy(g, 9, 9, s_x.at[g, 1 - zh], r_z.at[g], zh_peer)
        c.start()
        c.wait_recv()
        sends.append(c)
        total = s_x[g, zh] + r_z[g]
        for a in range(NBL):
            out_ref[a] = total[2 * a : 2 * a + 2]
        return sends

    for s in others:
        landed(0, s, send_mg, recv_mg).wait_recv()
    for a in range(NBL):
        cols = slice(a * BS, (a + 1) * BS)
        pg = (recv_mg[a].astype(F32) * dgelu[a]).astype(BF16)
        grad = dot_nn(pg, x_ref[:, cols]).astype(BF16)
        moved = dot_nt(by_core, grad).astype(BF16)
        g_all[0, a] = dot_nn(moved, placing).astype(BF16)
        ig_ref[:, cols] = dot_tn(pg, wm[a]).astype(BF16)
    sends = scatter_sum(0, fg_ref)

    for s in others:
        landed(1, s, send_act, recv_act).wait_recv()
    for d in range(NBL):
        cols = slice(d * BS, (d + 1) * BS)
        grad = dot_nn(recv_act[d], og_ref[:, cols]).astype(BF16)
        g_all[1, d] = dot_nn(by_core, grad).astype(BF16)
    sends += scatter_sum(1, lg_ref)

    for s in others:
        a2a(0, s, send_mg, recv_mg).wait_send()
        a2a(1, s, send_act, recv_act).wait_send()
    for c in sends:
        c.wait_send()


def per_device(tokens, first_blocks, latter_factor_blocks, block_perm, out_grad):
    vmem = pl.BlockSpec(memory_space=pltpu.VMEM)
    return pl.pallas_call(
        kernel,
        out_shape=(
            jax.ShapeDtypeStruct((NBL, 2, BS), F32),
            jax.ShapeDtypeStruct((NBL, 2, BS), F32),
            jax.ShapeDtypeStruct((ROWS, NBL * BS), BF16),
        ),
        in_specs=[vmem] * 5,
        out_specs=[vmem] * 3,
        scratch_shapes=[
            pltpu.VMEM((NBL, BS, BS), BF16),
            pltpu.VMEM((NBL, BS, ROWS), BF16),
            pltpu.VMEM((NBL, BS, ROWS), F32),
            pltpu.VMEM((NBL, NBL, 16, ROWS), BF16),
            pltpu.VMEM((NBL, BS, ROWS), BF16),
            pltpu.VMEM((NBL, NBL, 16, ROWS), BF16),
            pltpu.VMEM((NBL, BS, ROWS), BF16),
            pltpu.VMEM((2, NBL, BS, BS), BF16),
            pltpu.VMEM((2, NBL, 64, BS), BF16),
            pltpu.VMEM((2, NBL, 64, BS), BF16),
            pltpu.VMEM((2, 4, NBL, 16, BS), BF16),
            pltpu.VMEM((2, 2, 4, 16, BS), BF16),
            pltpu.VMEM((2, 4, 2, 16, BS), BF16),
            pltpu.VMEM((2, 2, 16, BS), F32),
            pltpu.VMEM((2, 16, BS), F32),
            pltpu.SemaphoreType.DMA((2, NBL)),
            pltpu.SemaphoreType.DMA((2, NBL)),
            pltpu.SemaphoreType.DMA((2, 10)),
            pltpu.SemaphoreType.DMA((2, 10)),
        ],
        compiler_params=pltpu.CompilerParams(
            collective_id=0, has_side_effects=True, vmem_limit_bytes=48 * 2**20
        ),
    )(tokens, first_blocks, latter_factor_blocks, block_perm.reshape(1, 64), out_grad)


def solution(mesh):
    return jax.shard_map(
        per_device,
        mesh=mesh,
        in_specs=(
            P("tok", "blk"),
            P("blk", None, None),
            P("blk", None, None),
            P(),
            P("tok", "blk"),
        ),
        out_specs=(P("blk", "tok", None), P("blk", "tok", None), P("tok", "blk")),
        check_vma=False,
    )
```

```python
import jax
import jax.numpy as jnp
from jax import lax
from jax.experimental import pallas as pl
from jax.experimental.pallas import tpu as pltpu
from jax.sharding import PartitionSpec as P

MESH = pl.DeviceIdType.MESH
F32 = jnp.float32
BF16 = jnp.bfloat16
ROWS = 256
BS = 128
NBL = 8
HOLD = True


def dot_nn(a, b):
    return lax.dot_general(a, b, (((1,), (0,)), ((), ())), preferred_element_type=F32)


def dot_nt(a, b):
    return lax.dot_general(a, b, (((1,), (1,)), ((), ())), preferred_element_type=F32)


def dot_tn(a, b):
    return lax.dot_general(a, b, (((0,), (0,)), ((), ())), preferred_element_type=F32)


def iota(dim):
    return lax.broadcasted_iota(jnp.int32, (BS, BS), dim)


def one_hot(hit):
    return jnp.where(hit, 1.0, 0.0).astype(BF16)


def kernel(
    x_hbm, w_hbm, l_hbm, perm_hbm, og_hbm,
    fg_ref, lg_ref, ig_ref,
    x_ref, w_ref, l_ref, perm_ref, og_ref, in_sem,
    wm, tmp, dgelu, send_mg, recv_mg, send_act, recv_act, part,
    g_core, r_core, s_core, r_y, s_y, r_x, s_x, r_z,
    a2a_send, a2a_recv, rs_send, rs_recv, edge_sem, open_sem,
):
    b = lax.axis_index("blk")
    t = lax.axis_index("tok")
    zh, x, y, core = t // 32, (t // 8) % 4, (t // 2) % 4, t % 2
    half, place = b // 4, b % 4

    def ring(at, k):
        return (at + k) % 4

    core_peer = (b, t + 1 - 2 * core)
    zh_peer = (b, t + 32 - 64 * zh)

    def y_peer(k):
        return (b, t + (ring(y, k) - y) * 2)

    def x_peer(k):
        return (b, t + (ring(x, k) - x) * 8)

    far = [(1 - half) * 4 + ring(place, k) for k in range(4)]
    near = [half * 4 + ring(place, k) for k in range(1, 4)]
    others = far + near

    at_edge = b == 7 - 7 * zh
    edge_peer = (7 - b, t + 32 - 64 * zh)

    def signal(sem, peer):
        pl.semaphore_signal(sem, inc=1, device_id=peer, device_id_type=MESH)

    barrier = pltpu.get_barrier_semaphore()
    peers = [(s, t) for s in others] + [core_peer]
    peers += [y_peer(k) for k in range(1, 4)] + [x_peer(k) for k in range(1, 4)]
    for peer in peers:
        signal(barrier, peer)

    @pl.when(at_edge)
    def _():
        signal(barrier, edge_peer)

    loads = [
        pltpu.make_async_copy(src, dst, in_sem.at[i])
        for i, (src, dst) in enumerate(
            (
                (og_hbm, og_ref),
                (l_hbm, l_ref),
                (w_hbm, w_ref),
                (x_hbm, x_ref),
                (perm_hbm, perm_ref),
            )
        )
    ]
    for load in loads:
        load.start()

    row, col = iota(0), iota(1)
    swap = one_hot(col == ((row >> 1) & 7) * 16 + (row >> 4) * 2 + (row & 1))

    def slab(s):
        return pl.ds(pl.multiple_of(s * 16, 16), 16)

    def a2a(phase, to, at, send, recv):
        return pltpu.make_async_remote_copy(
            src_ref=send.at[to],
            dst_ref=recv.at[:, slab(at), :],
            send_sem=a2a_send.at[phase, to],
            recv_sem=a2a_recv.at[phase, at],
            device_id=(to, t),
            device_id_type=MESH,
        )

    def mg_copy(to, at):
        return a2a(0, to, at, send_mg, recv_mg)

    def act_copy(to, at):
        return a2a(1, to, at, send_act, recv_act)

    def swapped(src, s):
        width = src.shape[-1]
        chunk = src[:, slab(s), :].reshape(BS, width)
        return dot_nn(swap, chunk).astype(BF16).reshape(NBL, 16, width)

    loads[0].wait()
    loads[1].wait()
    for d in range(NBL):
        cols = slice(d * BS, (d + 1) * BS)
        tmp[d] = dot_nt(l_ref[d], og_ref[:, cols]).astype(BF16)
    for at, s in enumerate(others):
        send_mg[s] = swapped(tmp, s)
        if at == 0:
            pl.semaphore_wait(barrier, len(peers) + jnp.where(at_edge, 1, 0))
        mg_copy(s, b).start()
    recv_mg[:, slab(b), :] = swapped(tmp, b)

    @pl.when(at_edge)
    def _():
        signal(edge_sem, edge_peer)

    for load in loads[2:]:
        load.wait()
    perm = jnp.broadcast_to(perm_ref[...].astype(F32), (16, 64)).astype(BF16)
    pair = one_hot(iota(1)[:64] // 2 == iota(0)[:64])
    target = dot_nn(perm, pair)[:1] * 2.0 + (iota(1)[:1] % 2).astype(F32)
    placing = one_hot(iota(0).astype(F32) == target)
    for a in range(NBL):
        cols = slice(a * BS, (a + 1) * BS)
        wm[a] = dot_nt(placing, w_ref[a]).astype(BF16)
        pre = dot_nt(wm[a], x_ref[:, cols])
        cdf = 0.5 * (1.0 + lax.erf(pre * 0.7071067811865476))
        tmp[a] = (pre * cdf).astype(BF16)
        dgelu[a] = cdf + pre * 0.3989422804014327 * jnp.exp(-0.5 * pre * pre)
    for s in near + far:
        send_act[s] = swapped(tmp, s)
    recv_act[:, slab(b), :] = swapped(tmp, b)
    for s in near:
        act_copy(s, b).start()
    for s in far:
        if HOLD:
            mg_copy(s, b).wait_send()
        act_copy(s, b).start()

    @pl.when(at_edge)
    def _():
        pl.semaphore_wait(edge_sem, 1)
        for k in range(1, 8):
            signal(open_sem, ((b + k) % 8, t))

    @pl.when(jnp.logical_not(at_edge))
    def _():
        pl.semaphore_wait(open_sem, 1)

    sends = []

    def copy(n, at_src, at_dst, src, dst, peer):
        return pltpu.make_async_remote_copy(
            src_ref=src,
            dst_ref=dst,
            send_sem=rs_send.at[n, at_src],
            recv_sem=rs_recv.at[n, at_dst],
            device_id=peer,
            device_id_type=MESH,
        )

    def plane_sum(n):
        c = copy(n, 0, 0, g_core.at[n, :, :, 1 - core], r_core.at[n], core_peer)
        c.start()
        c.wait_recv()
        sends.append(c)
        s_core[n] = (g_core[n, :, :, core].astype(F32) + r_core[n].astype(F32)).astype(
            BF16
        )
        for k in range(1, 4):
            to = ring(y, k)
            c = copy(n, 1 + to, 1 + y, s_core.at[n, :, to], r_y.at[n, y], y_peer(k))
            c.start()
            sends.append(c)
        total = s_core[n, :, y].astype(F32)
        for k in range(1, 4):
            at = ring(y, k)
            copy(
                n, 1 + at, 1 + at, s_core.at[n, :, at], r_y.at[n, at], y_peer(k)
            ).wait_recv()
            total = total + r_y[n, at].astype(F32)
        s_y[n] = total.astype(BF16)
        for k in range(1, 4):
            to = ring(x, k)
            c = copy(n, 5 + to, 5 + x, s_y.at[n, to], r_x.at[n, x], x_peer(k))
            c.start()
            sends.append(c)
        total = s_y[n, x].astype(F32)
        for k in range(1, 4):
            at = ring(x, k)
            copy(
                n, 5 + at, 5 + at, s_y.at[n, at], r_x.at[n, at], x_peer(k)
            ).wait_recv()
            total = total + r_x[n, at].astype(F32)
        return total

    def across(g):
        return copy(2 * g, 9, 9, s_x.at[g, 1 - zh], r_z.at[g], zh_peer)

    def finish(g, out_ref):
        across(g).wait_recv()
        total = s_x[g, zh] + r_z[g]
        for a in range(NBL):
            out_ref[a] = total[2 * a : 2 * a + 2]

    for s in others:
        mg_copy(s, s).wait_recv()
    for a in range(NBL):
        cols = slice(a * BS, (a + 1) * BS)
        pg = (recv_mg[a].astype(F32) * dgelu[a]).astype(BF16)
        grad = dot_nn(pg, x_ref[:, cols]).astype(BF16)
        part[a] = dot_tn(grad, placing).astype(BF16)
        ig_ref[:, cols] = dot_tn(pg, wm[a]).astype(BF16)
    for s in range(NBL):
        g_core[s // 4, s % 4] = swapped(part, s).reshape(4, 2, 16, BS)
    s_x[0, 0] = plane_sum(0)
    s_x[0, 1] = plane_sum(1)
    across(0).start()

    def second(which, sources, h):
        for s in sources:
            act_copy(s, s).wait_recv()
        rows = pl.ds(pl.multiple_of(h * 64, 64), 64)
        for d in range(NBL):
            cols = slice(d * BS, (d + 1) * BS)
            part[d, :64] = dot_nn(recv_act[d, rows, :], og_ref[:, cols]).astype(BF16)
        for s in range(4):
            g_core[which, s] = swapped(part, s).reshape(4, 2, 16, BS)
        s_x[1, h] = plane_sum(which)

    second(2, near, half)

    @pl.when(zh != half)
    def _():
        across(1).start()

    second(3, far, 1 - half)

    @pl.when(zh == half)
    def _():
        across(1).start()

    finish(0, fg_ref)
    finish(1, lg_ref)
    for s in others:
        if not HOLD:
            mg_copy(s, b).wait_send()
        act_copy(s, b).wait_send()
    if HOLD:
        for s in near:
            mg_copy(s, b).wait_send()
    for c in sends:
        c.wait_send()
    across(0).wait_send()
    across(1).wait_send()


def per_device(tokens, first_blocks, latter_factor_blocks, block_perm, out_grad):
    vmem = pl.BlockSpec(memory_space=pltpu.VMEM)
    hbm = pl.BlockSpec(memory_space=pltpu.HBM)
    return pl.pallas_call(
        kernel,
        out_shape=(
            jax.ShapeDtypeStruct((NBL, 2, BS), F32),
            jax.ShapeDtypeStruct((NBL, 2, BS), F32),
            jax.ShapeDtypeStruct((ROWS, NBL * BS), BF16),
        ),
        in_specs=[hbm] * 5,
        out_specs=[vmem] * 3,
        scratch_shapes=[
            pltpu.VMEM((ROWS, NBL * BS), BF16),
            pltpu.VMEM((NBL, BS, BS), BF16),
            pltpu.VMEM((NBL, BS, BS), BF16),
            pltpu.VMEM((1, 64), jnp.int32),
            pltpu.VMEM((ROWS, NBL * BS), BF16),
            pltpu.SemaphoreType.DMA((5,)),
            pltpu.VMEM((NBL, BS, BS), BF16),
            pltpu.VMEM((NBL, BS, ROWS), BF16),
            pltpu.VMEM((NBL, BS, ROWS), F32),
            pltpu.VMEM((NBL, NBL, 16, ROWS), BF16),
            pltpu.VMEM((NBL, BS, ROWS), BF16),
            pltpu.VMEM((NBL, NBL, 16, ROWS), BF16),
            pltpu.VMEM((NBL, BS, ROWS), BF16),
            pltpu.VMEM((NBL, BS, BS), BF16),
            pltpu.VMEM((4, 4, 4, 2, 16, BS), BF16),
            pltpu.VMEM((4, 4, 4, 16, BS), BF16),
            pltpu.VMEM((4, 4, 4, 16, BS), BF16),
            pltpu.VMEM((4, 4, 4, 16, BS), BF16),
            pltpu.VMEM((4, 4, 16, BS), BF16),
            pltpu.VMEM((4, 4, 16, BS), BF16),
            pltpu.VMEM((2, 2, 16, BS), F32),
            pltpu.VMEM((2, 16, BS), F32),
            pltpu.SemaphoreType.DMA((2, NBL)),
            pltpu.SemaphoreType.DMA((2, NBL)),
            pltpu.SemaphoreType.DMA((4, 10)),
            pltpu.SemaphoreType.DMA((4, 10)),
            pltpu.SemaphoreType.REGULAR,
            pltpu.SemaphoreType.REGULAR,
        ],
        compiler_params=pltpu.CompilerParams(
            collective_id=0, has_side_effects=True, vmem_limit_bytes=56 * 2**20
        ),
    )(tokens, first_blocks, latter_factor_blocks, block_perm.reshape(1, 64), out_grad)


def solution(mesh):
    return jax.shard_map(
        per_device,
        mesh=mesh,
        in_specs=(
            P("tok", "blk"),
            P("blk", None, None),
            P("blk", None, None),
            P(),
            P("tok", "blk"),
        ),
        out_specs=(P("blk", "tok", None), P("blk", "tok", None), P("tok", "blk")),
        check_vma=False,
    )
```

```python
import jax
import jax.numpy as jnp
from jax import lax
from jax.experimental import pallas as pl
from jax.experimental.pallas import tpu as pltpu
from jax.sharding import PartitionSpec as P

MESH = pl.DeviceIdType.MESH
F32 = jnp.float32
BF16 = jnp.bfloat16
ROWS = 256
BS = 128
NBL = 8
HOLD = True


def dot_nn(a, b):
    return lax.dot_general(a, b, (((1,), (0,)), ((), ())), preferred_element_type=F32)


def dot_nt(a, b):
    return lax.dot_general(a, b, (((1,), (1,)), ((), ())), preferred_element_type=F32)


def dot_tn(a, b):
    return lax.dot_general(a, b, (((0,), (0,)), ((), ())), preferred_element_type=F32)


def iota(dim):
    return lax.broadcasted_iota(jnp.int32, (BS, BS), dim)


def one_hot(hit):
    return jnp.where(hit, 1.0, 0.0).astype(BF16)


def kernel(
    x_hbm, w_hbm, l_hbm, perm_hbm, og_hbm,
    fg_ref, lg_ref, ig_ref,
    x_ref, w_ref, l_ref, perm_ref, og_ref, in_sem,
    wm, tmp, dgelu, send_mg, recv_mg, send_act, recv_act, part,
    g_early, rq_early, sq_early, rx_early, g_late, rq_late, sq_late, rx_late, s_x, r_z,
    a2a_send, a2a_recv, rs_send, rs_recv, edge_sem, open_sem,
):
    b = lax.axis_index("blk")
    t = lax.axis_index("tok")
    zh, x, q = t // 32, (t // 8) % 4, t % 8
    half, place = b // 4, b % 4

    def ring(at, k):
        return (at + k) % 4

    zh_peer = (b, t + 32 - 64 * zh)

    def q_peer(k):
        return (b, t + (q + k) % 8 - q)

    def x_peer(k):
        return (b, t + (ring(x, k) - x) * 8)

    far = [(1 - half) * 4 + ring(place, k) for k in range(4)]
    near = [half * 4 + ring(place, k) for k in range(1, 4)]
    others = far + near

    at_edge = b == 7 - 7 * zh
    edge_peer = (7 - b, t + 32 - 64 * zh)

    def signal(sem, peer):
        pl.semaphore_signal(sem, inc=1, device_id=peer, device_id_type=MESH)

    barrier = pltpu.get_barrier_semaphore()
    peers = [(s, t) for s in others]
    peers += [q_peer(k) for k in range(1, 8)] + [x_peer(k) for k in range(1, 4)]
    for peer in peers:
        signal(barrier, peer)

    @pl.when(at_edge)
    def _():
        signal(barrier, edge_peer)

    loads = [
        pltpu.make_async_copy(src, dst, in_sem.at[i])
        for i, (src, dst) in enumerate(
            (
                (og_hbm, og_ref),
                (l_hbm, l_ref),
                (w_hbm, w_ref),
                (x_hbm, x_ref),
                (perm_hbm, perm_ref),
            )
        )
    ]
    for load in loads:
        load.start()

    row, col = iota(0), iota(1)
    swap = one_hot(col == ((row >> 1) & 7) * 16 + (row >> 4) * 2 + (row & 1))

    def slab(s):
        return pl.ds(pl.multiple_of(s * 16, 16), 16)

    def a2a(phase, to, at, send, recv):
        return pltpu.make_async_remote_copy(
            src_ref=send.at[to],
            dst_ref=recv.at[:, slab(at), :],
            send_sem=a2a_send.at[phase, to],
            recv_sem=a2a_recv.at[phase, at],
            device_id=(to, t),
            device_id_type=MESH,
        )

    def mg_copy(to, at):
        return a2a(0, to, at, send_mg, recv_mg)

    def act_copy(to, at):
        return a2a(1, to, at, send_act, recv_act)

    def swapped(src, s):
        width = src.shape[-1]
        chunk = src[:, slab(s), :].reshape(BS, width)
        return dot_nn(swap, chunk).astype(BF16).reshape(NBL, 16, width)

    loads[0].wait()
    loads[1].wait()
    for d in range(NBL):
        cols = slice(d * BS, (d + 1) * BS)
        tmp[d] = dot_nt(l_ref[d], og_ref[:, cols]).astype(BF16)
    for at, s in enumerate(others):
        send_mg[s] = swapped(tmp, s)
        if at == 0:
            pl.semaphore_wait(barrier, len(peers) + jnp.where(at_edge, 1, 0))
        mg_copy(s, b).start()
    recv_mg[:, slab(b), :] = swapped(tmp, b)

    @pl.when(at_edge)
    def _():
        signal(edge_sem, edge_peer)

    for load in loads[2:]:
        load.wait()
    perm = jnp.broadcast_to(perm_ref[...].astype(F32), (16, 64)).astype(BF16)
    pair = one_hot(iota(1)[:64] // 2 == iota(0)[:64])
    target = dot_nn(perm, pair)[:1] * 2.0 + (iota(1)[:1] % 2).astype(F32)
    placing = one_hot(iota(0).astype(F32) == target)
    for a in range(NBL):
        cols = slice(a * BS, (a + 1) * BS)
        wm[a] = dot_nt(placing, w_ref[a]).astype(BF16)
        pre = dot_nt(wm[a], x_ref[:, cols])
        cdf = 0.5 * (1.0 + lax.erf(pre * 0.7071067811865476))
        tmp[a] = (pre * cdf).astype(BF16)
        dgelu[a] = cdf + pre * 0.3989422804014327 * jnp.exp(-0.5 * pre * pre)
    for s in near + far:
        send_act[s] = swapped(tmp, s)
    recv_act[:, slab(b), :] = swapped(tmp, b)
    for s in near:
        act_copy(s, b).start()
    for s in far:
        if HOLD:
            mg_copy(s, b).wait_send()
        act_copy(s, b).start()

    @pl.when(at_edge)
    def _():
        pl.semaphore_wait(edge_sem, 1)
        for k in range(1, 8):
            signal(open_sem, ((b + k) % 8, t))

    @pl.when(jnp.logical_not(at_edge))
    def _():
        pl.semaphore_wait(open_sem, 1)

    sends = []

    def copy(n, at_src, at_dst, src, dst, peer):
        return pltpu.make_async_remote_copy(
            src_ref=src,
            dst_ref=dst,
            send_sem=rs_send.at[n, at_src],
            recv_sem=rs_recv.at[n, at_dst],
            device_id=peer,
            device_id_type=MESH,
        )

    def plane_sum(n, g, r_q, s_q, r_x):
        for k in range(1, 8):
            to = (q + k) % 8
            c = copy(n, to, q, g.at[:, :, to], r_q.at[q], q_peer(k))
            c.start()
            sends.append(c)
        total = g[:, :, q].astype(F32)
        for k in range(1, 8):
            at = (q + k) % 8
            copy(n, at, at, g.at[:, :, at], r_q.at[at], q_peer(k)).wait_recv()
            total = total + r_q[at].astype(F32)
        s_q[...] = total.astype(BF16)
        for k in range(1, 4):
            to = ring(x, k)
            c = copy(n, 8 + to, 8 + x, s_q.at[:, to], r_x.at[x], x_peer(k))
            c.start()
            sends.append(c)
        total = s_q[:, x].astype(F32)
        for k in range(1, 4):
            at = ring(x, k)
            copy(n, 8 + at, 8 + at, s_q.at[:, at], r_x.at[at], x_peer(k)).wait_recv()
            total = total + r_x[at].astype(F32)
        return total

    def across(g):
        return copy(g, 12, 12, s_x.at[g, 1 - zh], r_z.at[g], zh_peer)

    def finish(g, out_ref):
        across(g).wait_recv()
        total = s_x[g, zh] + r_z[g]
        for a in range(NBL):
            out_ref[a] = total[2 * a : 2 * a + 2]

    def second(sources, h, store):
        for s in sources:
            act_copy(s, s).wait_recv()
        rows = pl.ds(pl.multiple_of(h * 64, 64), 64)
        for d in range(NBL):
            cols = slice(d * BS, (d + 1) * BS)
            part[d, :64] = dot_nn(recv_act[d, rows, :], og_ref[:, cols]).astype(BF16)
        for s in range(4):
            store[s] = swapped(part, s).reshape(8, 16, BS)

    for s in others:
        mg_copy(s, s).wait_recv()
    for a in range(NBL):
        cols = slice(a * BS, (a + 1) * BS)
        pg = (recv_mg[a].astype(F32) * dgelu[a]).astype(BF16)
        tmp[a] = pg
        grad = dot_nn(pg, x_ref[:, cols]).astype(BF16)
        part[a] = dot_tn(grad, placing).astype(BF16)
    for s in range(NBL):
        g_early[s // 4, s % 4] = swapped(part, s).reshape(8, 16, BS)
    second(near, half, g_early.at[2])
    total = plane_sum(0, g_early, rq_early, sq_early, rx_early)
    s_x[0] = total[:2]
    s_x[1, half] = total[2]
    across(0).start()

    @pl.when(zh != half)
    def _():
        across(1).start()

    for a in range(NBL):
        cols = slice(a * BS, (a + 1) * BS)
        ig_ref[:, cols] = dot_tn(tmp[a], wm[a]).astype(BF16)

    second(far, 1 - half, g_late.at[0])
    s_x[1, 1 - half] = plane_sum(1, g_late, rq_late, sq_late, rx_late)[0]

    @pl.when(zh == half)
    def _():
        across(1).start()

    finish(0, fg_ref)
    finish(1, lg_ref)
    for s in others:
        if not HOLD:
            mg_copy(s, b).wait_send()
        act_copy(s, b).wait_send()
    if HOLD:
        for s in near:
            mg_copy(s, b).wait_send()
    for c in sends:
        c.wait_send()
    across(0).wait_send()
    across(1).wait_send()


def per_device(tokens, first_blocks, latter_factor_blocks, block_perm, out_grad):
    vmem = pl.BlockSpec(memory_space=pltpu.VMEM)
    hbm = pl.BlockSpec(memory_space=pltpu.HBM)
    tokens, first_blocks, latter_factor_blocks, block_perm, out_grad = [pltpu.with_memory_space_constraint(v, pltpu.HBM) for v in (tokens, first_blocks, latter_factor_blocks, block_perm.reshape(1, 64), out_grad)]
    return pl.pallas_call(
        kernel,
        out_shape=(
            jax.ShapeDtypeStruct((NBL, 2, BS), F32),
            jax.ShapeDtypeStruct((NBL, 2, BS), F32),
            jax.ShapeDtypeStruct((ROWS, NBL * BS), BF16),
        ),
        in_specs=[hbm] * 5,
        out_specs=[vmem] * 3,
        scratch_shapes=[
            pltpu.VMEM((ROWS, NBL * BS), BF16),
            pltpu.VMEM((NBL, BS, BS), BF16),
            pltpu.VMEM((NBL, BS, BS), BF16),
            pltpu.VMEM((1, 64), jnp.int32),
            pltpu.VMEM((ROWS, NBL * BS), BF16),
            pltpu.SemaphoreType.DMA((5,)),
            pltpu.VMEM((NBL, BS, BS), BF16),
            pltpu.VMEM((NBL, BS, ROWS), BF16),
            pltpu.VMEM((NBL, BS, ROWS), F32),
            pltpu.VMEM((NBL, NBL, 16, ROWS), BF16),
            pltpu.VMEM((NBL, BS, ROWS), BF16),
            pltpu.VMEM((NBL, NBL, 16, ROWS), BF16),
            pltpu.VMEM((NBL, BS, ROWS), BF16),
            pltpu.VMEM((NBL, BS, BS), BF16),
            pltpu.VMEM((3, 4, 8, 16, BS), BF16),
            pltpu.VMEM((8, 3, 4, 16, BS), BF16),
            pltpu.VMEM((3, 4, 16, BS), BF16),
            pltpu.VMEM((4, 3, 16, BS), BF16),
            pltpu.VMEM((1, 4, 8, 16, BS), BF16),
            pltpu.VMEM((8, 1, 4, 16, BS), BF16),
            pltpu.VMEM((1, 4, 16, BS), BF16),
            pltpu.VMEM((4, 1, 16, BS), BF16),
            pltpu.VMEM((2, 2, 16, BS), F32),
            pltpu.VMEM((2, 16, BS), F32),
            pltpu.SemaphoreType.DMA((2, NBL)),
            pltpu.SemaphoreType.DMA((2, NBL)),
            pltpu.SemaphoreType.DMA((2, 13)),
            pltpu.SemaphoreType.DMA((2, 13)),
            pltpu.SemaphoreType.REGULAR,
            pltpu.SemaphoreType.REGULAR,
        ],
        compiler_params=pltpu.CompilerParams(
            collective_id=0, has_side_effects=True, vmem_limit_bytes=24 * 2**20
        ),
    )(tokens, first_blocks, latter_factor_blocks, block_perm, out_grad)


def solution(mesh):
    return jax.shard_map(
        per_device,
        mesh=mesh,
        in_specs=(
            P("tok", "blk"),
            P("blk", None, None),
            P("blk", None, None),
            P(),
            P("tok", "blk"),
        ),
        out_specs=(P("blk", "tok", None), P("blk", "tok", None), P("tok", "blk")),
        check_vma=False,
    )
```

```python
import jax
import jax.numpy as jnp
from jax import lax
from jax.experimental import pallas as pl
from jax.experimental.pallas import tpu as pltpu
from jax.sharding import PartitionSpec as P

MESH = pl.DeviceIdType.MESH
F32 = jnp.float32
BF16 = jnp.bfloat16
ROWS = 256
BS = 128
NBL = 8


def dot_nn(a, b):
    return lax.dot_general(a, b, (((1,), (0,)), ((), ())), preferred_element_type=F32)


def dot_nt(a, b):
    return lax.dot_general(a, b, (((1,), (1,)), ((), ())), preferred_element_type=F32)


def dot_tn(a, b):
    return lax.dot_general(a, b, (((0,), (0,)), ((), ())), preferred_element_type=F32)


def iota(dim):
    return lax.broadcasted_iota(jnp.int32, (BS, BS), dim)


def one_hot(hit):
    return jnp.where(hit, 1.0, 0.0).astype(BF16)


def kernel(
    x_hbm, w_hbm, l_hbm, perm_hbm, og_hbm,
    fg_ref, lg_ref, ig_ref,
    x_ref, w_ref, l_ref, perm_ref, og_ref, in_sem,
    wm, tmp, act, dgelu, send_mg, recv_mg, send_act, recv_act, part,
    g_early, rq_early, sq_early, g_late, rq_late, sq_late, r_last,
    a2a_send, a2a_recv, rs_send, rs_recv, last_send, last_recv, edge_sem, open_sem, open_x_sem, up_sem, down_sem,
):
    b = lax.axis_index("blk")
    t = lax.axis_index("tok")
    zh, x, q = t // 32, (t // 8) % 4, t % 8
    half, place = b // 4, b % 4

    def ring(at, k):
        return (at + k) % 4

    zh_peer = (b, t + 32 - 64 * zh)

    def q_peer(k):
        return (b, t + (q + k) % 8 - q)

    def x_peer(k):
        return (b, t + (ring(x, k) - x) * 8)

    far = [(1 - half) * 4 + ring(place, k) for k in range(4)]
    near = [half * 4 + ring(place, k) for k in range(1, 4)]
    others = far + near

    at_edge = b == 7 - 7 * zh
    edge_peer = (7 - b, t + 32 - 64 * zh)

    def signal(sem, peer):
        pl.semaphore_signal(sem, inc=1, device_id=peer, device_id_type=MESH)

    barrier = pltpu.get_barrier_semaphore()
    for peer in [q_peer(k) for k in range(1, 8)] + [x_peer(k) for k in range(1, 4)]:
        signal(barrier, peer)

    @pl.when(b > 0)
    def _():
        signal(barrier, (b - 1, t))

    @pl.when(b < 7)
    def _():
        signal(barrier, (b + 1, t))

    @pl.when(at_edge)
    def _():
        signal(barrier, edge_peer)

    loads = [
        pltpu.make_async_copy(src, dst, in_sem.at[i])
        for i, (src, dst) in enumerate(
            (
                (og_hbm, og_ref),
                (l_hbm, l_ref),
                (w_hbm, w_ref),
                (x_hbm, x_ref),
                (perm_hbm, perm_ref),
            )
        )
    ]
    for load in loads:
        load.start()

    row, col = iota(0), iota(1)
    swap = one_hot(col == ((row >> 1) & 7) * 16 + (row >> 4) * 2 + (row & 1))

    def slab(s):
        return pl.ds(pl.multiple_of(s * 16, 16), 16)

    def a2a(phase, to, at, send, recv):
        return pltpu.make_async_remote_copy(
            src_ref=send.at[to],
            dst_ref=recv.at[:, slab(at), :],
            send_sem=a2a_send.at[phase, to],
            recv_sem=a2a_recv.at[phase, at],
            device_id=(to, t),
            device_id_type=MESH,
        )

    def mg_copy(to, at):
        return a2a(0, to, at, send_mg, recv_mg)

    def act_copy(to, at):
        return a2a(1, to, at, send_act, recv_act)

    def swapped(src, s):
        width = src.shape[-1]
        chunk = src[:, slab(s), :].reshape(BS, width)
        return dot_nn(swap, chunk).astype(BF16).reshape(NBL, 16, width)

    loads[0].wait()
    loads[1].wait()
    for d in range(NBL):
        cols = slice(d * BS, (d + 1) * BS)
        tmp[d] = dot_nt(l_ref[d], og_ref[:, cols]).astype(BF16)

    def entered(k):
        up, down = b + k, b - k

        @pl.when(down >= 0)
        def _():
            if k > 1:
                pl.semaphore_wait(down_sem.at[k], 1)
            if k < 7:

                @pl.when(b < 7)
                def _():
                    signal(down_sem.at[k + 1], (b + 1, t))

            send_mg[down] = swapped(tmp, down)
            mg_copy(down, b).start()

        @pl.when(up < 8)
        def _():
            if k > 1:
                pl.semaphore_wait(up_sem.at[k], 1)
            if k < 7:

                @pl.when(b > 0)
                def _():
                    signal(up_sem.at[k + 1], (b - 1, t))

            send_mg[up] = swapped(tmp, up)
            mg_copy(up, b).start()

    def activation(a):
        cols = slice(a * BS, (a + 1) * BS)
        wm[a] = dot_nt(placing, w_ref[a]).astype(BF16)
        pre = dot_nt(wm[a], x_ref[:, cols])
        cdf = 0.5 * (1.0 + lax.erf(pre * 0.7071067811865476))
        act[a] = (pre * cdf).astype(BF16)
        dgelu[a] = cdf + pre * 0.3989422804014327 * jnp.exp(-0.5 * pre * pre)

    pl.semaphore_wait(
        barrier, 10 + jnp.where(b > 0, 1, 0) + jnp.where(b < 7, 1, 0) + jnp.where(at_edge, 1, 0)
    )
    entered(1)
    for load in loads[2:]:
        load.wait()
    perm = jnp.broadcast_to(perm_ref[...].astype(F32), (16, 64)).astype(BF16)
    pair = one_hot(iota(1)[:64] // 2 == iota(0)[:64])
    target = dot_nn(perm, pair)[:1] * 2.0 + (iota(1)[:1] % 2).astype(F32)
    placing = one_hot(iota(0).astype(F32) == target)
    for k in range(2, 6):
        activation(2 * k - 4)
        activation(2 * k - 3)
        entered(k)
    entered(6)
    entered(7)
    recv_mg[:, slab(b), :] = swapped(tmp, b)

    @pl.when(at_edge)
    def _():
        signal(edge_sem, edge_peer)

    for s in near:
        send_act[s] = swapped(act, s)
        act_copy(s, b).start()
    for s in far:
        send_act[s] = swapped(act, s)
    recv_act[:, slab(b), :] = swapped(act, b)

    @pl.when(at_edge)
    def _():
        pl.semaphore_wait(edge_sem, 1)
        for k in range(1, 8):
            signal(open_sem, ((b + k) % 8, t))

    @pl.when(jnp.logical_not(at_edge))
    def _():
        pl.semaphore_wait(open_sem, 1)

    for k in range(1, 4):
        signal(open_x_sem, x_peer(k))

    for s in others:
        mg_copy(s, s).wait_recv()
    for s in far:
        act_copy(s, b).start()

    sends = []

    def copy(send_sem, recv_sem, n, at_src, at_dst, src, dst, peer):
        return pltpu.make_async_remote_copy(
            src_ref=src,
            dst_ref=dst,
            send_sem=send_sem.at[n, at_src],
            recv_sem=recv_sem.at[n, at_dst],
            device_id=peer,
            device_id_type=MESH,
        )

    def q_sum(n, g, r_q, s_q):
        for k in range(1, 8):
            to = (q + k) % 8
            c = copy(rs_send, rs_recv, n, to, q, g.at[:, :, to], r_q.at[q], q_peer(k))
            c.start()
            sends.append(c)
        total = g[:, :, q].astype(F32)
        for k in range(1, 8):
            at = (q + k) % 8
            copy(
                rs_send, rs_recv, n, at, at, g.at[:, :, at], r_q.at[at], q_peer(k)
            ).wait_recv()
            total = total + r_q[at].astype(F32)
        s_q[...] = total.astype(BF16)

    def last_copy(u, g, h, k, src):
        to = ring(x, k)
        return pltpu.make_async_remote_copy(
            src_ref=src.at[to],
            dst_ref=r_last.at[g, zh * 4 + x],
            send_sem=last_send.at[u, to],
            recv_sem=last_recv.at[g, zh * 4 + x],
            device_id=(b, h * 32 + to * 8 + q),
            device_id_type=MESH,
        )

    def last_start(*which):
        for k in range(1, 4):
            last_copy(*which[:3], k, which[3]).start()

        @pl.when(zh != which[2])
        def _():
            last_copy(*which[:3], 0, which[3]).start()

        @pl.when(zh == which[2])
        def _():
            r_last[which[1], zh * 4 + x] = which[3][x]

    def last_drain(*which):
        for k in range(1, 4):
            last_copy(*which[:3], k, which[3]).wait_send()

        @pl.when(zh != which[2])
        def _():
            last_copy(*which[:3], 0, which[3]).wait_send()

    def finish(g, out_ref):
        for k in range(1, 8):
            at = (zh * 4 + x + k) % 8
            pltpu.make_async_remote_copy(
                src_ref=r_last.at[g, at],
                dst_ref=r_last.at[g, at],
                send_sem=last_send.at[g, 0],
                recv_sem=last_recv.at[g, at],
                device_id=zh_peer,
                device_id_type=MESH,
            ).wait_recv()
        total = r_last[g, 0].astype(F32)
        for at in range(1, 8):
            total = total + r_last[g, at].astype(F32)
        for a in range(NBL):
            out_ref[a] = total[2 * a : 2 * a + 2]

    def second(sources, h, store):
        for s in sources:
            act_copy(s, s).wait_recv()
        rows = pl.ds(pl.multiple_of(h * 64, 64), 64)
        for d in range(NBL):
            cols = slice(d * BS, (d + 1) * BS)
            part[d, :64] = dot_nn(recv_act[d, rows, :], og_ref[:, cols]).astype(BF16)
        for s in range(4):
            store[s] = swapped(part, s).reshape(8, 16, BS)

    for a in range(NBL):
        cols = slice(a * BS, (a + 1) * BS)
        pg = (recv_mg[a].astype(F32) * dgelu[a]).astype(BF16)
        tmp[a] = pg
        grad = dot_nn(pg, x_ref[:, cols]).astype(BF16)
        part[a] = dot_tn(grad, placing).astype(BF16)
    for s in range(NBL):
        g_early[s // 4, s % 4] = swapped(part, s).reshape(8, 16, BS)
    second(near, half, g_early.at[2])
    q_sum(0, g_early, rq_early, sq_early)
    pl.semaphore_wait(open_x_sem, 3)
    lasts = [
        (0, 0, 0, sq_early.at[0]),
        (1, 0, 1, sq_early.at[1]),
        (2, 1, half, sq_early.at[2]),
        (3, 1, 1 - half, sq_late.at[0]),
    ]
    for last in lasts[:3]:
        last_start(*last)

    for a in range(NBL):
        cols = slice(a * BS, (a + 1) * BS)
        ig_ref[:, cols] = dot_tn(tmp[a], wm[a]).astype(BF16)

    second(far, 1 - half, g_late.at[0])
    q_sum(1, g_late, rq_late, sq_late)
    last_start(*lasts[3])

    finish(0, fg_ref)
    finish(1, lg_ref)
    for s in others:
        mg_copy(s, b).wait_send()
        act_copy(s, b).wait_send()
    for c in sends:
        c.wait_send()
    for last in lasts:
        last_drain(*last)


def per_device(tokens, first_blocks, latter_factor_blocks, block_perm, out_grad):
    vmem = pl.BlockSpec(memory_space=pltpu.VMEM)
    hbm = pl.BlockSpec(memory_space=pltpu.HBM)
    tokens, first_blocks, latter_factor_blocks, block_perm, out_grad = [pltpu.with_memory_space_constraint(v, pltpu.HBM) for v in (tokens, first_blocks, latter_factor_blocks, block_perm.reshape(1, 64), out_grad)]
    return pl.pallas_call(
        kernel,
        out_shape=(
            jax.ShapeDtypeStruct((NBL, 2, BS), F32),
            jax.ShapeDtypeStruct((NBL, 2, BS), F32),
            jax.ShapeDtypeStruct((ROWS, NBL * BS), BF16),
        ),
        in_specs=[hbm] * 5,
        out_specs=[vmem] * 3,
        scratch_shapes=[
            pltpu.VMEM((ROWS, NBL * BS), BF16),
            pltpu.VMEM((NBL, BS, BS), BF16),
            pltpu.VMEM((NBL, BS, BS), BF16),
            pltpu.VMEM((1, 64), jnp.int32),
            pltpu.VMEM((ROWS, NBL * BS), BF16),
            pltpu.SemaphoreType.DMA((5,)),
            pltpu.VMEM((NBL, BS, BS), BF16),
            pltpu.VMEM((NBL, BS, ROWS), BF16),
            pltpu.VMEM((NBL, BS, ROWS), BF16),
            pltpu.VMEM((NBL, BS, ROWS), F32),
            pltpu.VMEM((NBL, NBL, 16, ROWS), BF16),
            pltpu.VMEM((NBL, BS, ROWS), BF16),
            pltpu.VMEM((NBL, NBL, 16, ROWS), BF16),
            pltpu.VMEM((NBL, BS, ROWS), BF16),
            pltpu.VMEM((NBL, BS, BS), BF16),
            pltpu.VMEM((3, 4, 8, 16, BS), BF16),
            pltpu.VMEM((8, 3, 4, 16, BS), BF16),
            pltpu.VMEM((3, 4, 16, BS), BF16),
            pltpu.VMEM((1, 4, 8, 16, BS), BF16),
            pltpu.VMEM((8, 1, 4, 16, BS), BF16),
            pltpu.VMEM((1, 4, 16, BS), BF16),
            pltpu.VMEM((2, 8, 16, BS), BF16),
            pltpu.SemaphoreType.DMA((2, NBL)),
            pltpu.SemaphoreType.DMA((2, NBL)),
            pltpu.SemaphoreType.DMA((2, 8)),
            pltpu.SemaphoreType.DMA((2, 8)),
            pltpu.SemaphoreType.DMA((4, 4)),
            pltpu.SemaphoreType.DMA((2, 8)),
            pltpu.SemaphoreType.REGULAR,
            pltpu.SemaphoreType.REGULAR,
            pltpu.SemaphoreType.REGULAR,
            pltpu.SemaphoreType.REGULAR((8,)),
            pltpu.SemaphoreType.REGULAR((8,)),
        ],
        compiler_params=pltpu.CompilerParams(
            collective_id=0, has_side_effects=True, vmem_limit_bytes=24 * 2**20
        ),
    )(tokens, first_blocks, latter_factor_blocks, block_perm, out_grad)


def solution(mesh):
    return jax.shard_map(
        per_device,
        mesh=mesh,
        in_specs=(
            P("tok", "blk"),
            P("blk", None, None),
            P("blk", None, None),
            P(),
            P("tok", "blk"),
        ),
        out_specs=(P("blk", "tok", None), P("blk", "tok", None), P("tok", "blk")),
        check_vma=False,
    )
```

```python
import jax
import jax.numpy as jnp
from jax import lax
from jax.experimental import pallas as pl
from jax.experimental.pallas import tpu as pltpu
from jax.sharding import PartitionSpec as P

MESH = pl.DeviceIdType.MESH
F32 = jnp.float32
BF16 = jnp.bfloat16
ROWS = 256
BS = 128
NBL = 8


def dot_nn(a, b):
    return lax.dot_general(a, b, (((1,), (0,)), ((), ())), preferred_element_type=F32)


def dot_nt(a, b):
    return lax.dot_general(a, b, (((1,), (1,)), ((), ())), preferred_element_type=F32)


def dot_tn(a, b):
    return lax.dot_general(a, b, (((0,), (0,)), ((), ())), preferred_element_type=F32)


def iota(dim):
    return lax.broadcasted_iota(jnp.int32, (BS, BS), dim)


def one_hot(hit):
    return jnp.where(hit, 1.0, 0.0).astype(BF16)


def kernel(
    x_hbm, w_hbm, l_hbm, perm_hbm, og_hbm,
    fg_ref, lg_ref, ig_ref,
    x_ref, w_ref, l_ref, perm_ref, og_ref, in_sem,
    wm, tmp, act, dgelu, send_mg, recv_mg, send_act, recv_act, part,
    g_early, rq_early, sq_early, g_late, rq_late, sq_late, r_last,
    a2a_send, a2a_recv, rs_send, rs_recv, last_send, last_recv, edge_sem, edge_x_sem, open_sem, up_sem, down_sem,
):
    b = lax.axis_index("blk")
    t = lax.axis_index("tok")
    zh, x, q = t // 32, (t // 8) % 4, t % 8
    half, place = b // 4, b % 4

    def ring(at, k):
        return (at + k) % 4

    zh_peer = (b, t + 32 - 64 * zh)

    def q_peer(k):
        return (b, t + (q + k) % 8 - q)

    def x_peer(k):
        return (b, t + (ring(x, k) - x) * 8)

    far = [half * (3 - k) + (1 - half) * (4 + k) for k in range(4)]
    near = [half * 4 + ring(place, k) for k in range(1, 4)]
    others = far + near

    at_edge = b == 7 - 7 * zh
    edge_peer = (7 - b, t + 32 - 64 * zh)

    def signal(sem, peer):
        pl.semaphore_signal(sem, inc=1, device_id=peer, device_id_type=MESH)

    barrier = pltpu.get_barrier_semaphore()
    plane = [q_peer(k) for k in range(1, 8)] + [x_peer(k) for k in range(1, 4)]

    @pl.when(b > 0)
    def _():
        signal(barrier, (b - 1, t))

    @pl.when(b < 7)
    def _():
        signal(barrier, (b + 1, t))

    @pl.when(at_edge)
    def _():
        for peer in [*plane, edge_peer]:
            signal(barrier, peer)

    loads = [
        pltpu.make_async_copy(src, dst, in_sem.at[i])
        for i, (src, dst) in enumerate(
            (
                (og_hbm, og_ref),
                (l_hbm, l_ref),
                (w_hbm, w_ref),
                (x_hbm, x_ref),
                (perm_hbm, perm_ref),
            )
        )
    ]
    for load in loads:
        load.start()

    row, col = iota(0), iota(1)
    swap = one_hot(col == ((row >> 1) & 7) * 16 + (row >> 4) * 2 + (row & 1))

    def slab(s):
        return pl.ds(pl.multiple_of(s * 16, 16), 16)

    def a2a(phase, to, at, send, recv):
        return pltpu.make_async_remote_copy(
            src_ref=send.at[to],
            dst_ref=recv.at[:, slab(at), :],
            send_sem=a2a_send.at[phase, to],
            recv_sem=a2a_recv.at[phase, at],
            device_id=(to, t),
            device_id_type=MESH,
        )

    def mg_copy(to, at):
        return a2a(0, to, at, send_mg, recv_mg)

    def act_copy(to, at):
        return a2a(1, to, at, send_act, recv_act)

    def swapped(src, s):
        width = src.shape[-1]
        chunk = src[:, slab(s), :].reshape(BS, width)
        return dot_nn(swap, chunk).astype(BF16).reshape(NBL, 16, width)

    loads[0].wait()
    loads[1].wait()
    for d in range(NBL):
        cols = slice(d * BS, (d + 1) * BS)
        tmp[d] = dot_nt(l_ref[d], og_ref[:, cols]).astype(BF16)

    def entered(k):
        up, down = b + k, b - k

        @pl.when(down >= 0)
        def _():
            if k > 1:
                pl.semaphore_wait(down_sem.at[k], 1)
            if k < 7:

                @pl.when(b < 7)
                def _():
                    signal(down_sem.at[k + 1], (b + 1, t))

            send_mg[down] = swapped(tmp, down)
            mg_copy(down, b).start()

        @pl.when(up < 8)
        def _():
            if k > 1:
                pl.semaphore_wait(up_sem.at[k], 1)
            if k < 7:

                @pl.when(b > 0)
                def _():
                    signal(up_sem.at[k + 1], (b - 1, t))

            send_mg[up] = swapped(tmp, up)
            mg_copy(up, b).start()

    def activation(a):
        cols = slice(a * BS, (a + 1) * BS)
        wm[a] = dot_nt(placing, w_ref[a]).astype(BF16)
        pre = dot_nt(wm[a], x_ref[:, cols])
        cdf = 0.5 * (1.0 + lax.erf(pre * 0.7071067811865476))
        act[a] = (pre * cdf).astype(BF16)
        dgelu[a] = cdf + pre * 0.3989422804014327 * jnp.exp(-0.5 * pre * pre)

    pl.semaphore_wait(
        barrier,
        jnp.where(b > 0, 1, 0) + jnp.where(b < 7, 1, 0) + jnp.where(at_edge, 11, 0),
    )
    entered(1)
    for load in loads[2:]:
        load.wait()
    perm = jnp.broadcast_to(perm_ref[...].astype(F32), (16, 64)).astype(BF16)
    pair = one_hot(iota(1)[:64] // 2 == iota(0)[:64])
    target = dot_nn(perm, pair)[:1] * 2.0 + (iota(1)[:1] % 2).astype(F32)
    placing = one_hot(iota(0).astype(F32) == target)
    for k in range(2, 6):
        activation(2 * k - 4)
        activation(2 * k - 3)
        entered(k)
    entered(6)
    entered(7)
    recv_mg[:, slab(b), :] = swapped(tmp, b)

    @pl.when(at_edge)
    def _():
        for peer in [*plane, edge_peer]:
            signal(edge_sem, peer)

    for s in near:
        send_act[s] = swapped(act, s)
        act_copy(s, b).start()
    for s in far:
        send_act[s] = swapped(act, s)
    recv_act[:, slab(b), :] = swapped(act, b)

    for s in far:
        act_copy(s, b).start()

    @pl.when(at_edge)
    def _():
        pl.semaphore_wait(edge_sem, 11)
        for k in range(1, 4):
            signal(edge_x_sem, x_peer(k))
        pl.semaphore_wait(edge_x_sem, 3)
        for k in range(1, 8):
            signal(open_sem, ((b + k) % 8, t))

    @pl.when(jnp.logical_not(at_edge))
    def _():
        pl.semaphore_wait(open_sem, 1)

    for s in others:
        mg_copy(s, s).wait_recv()

    sends = []

    def copy(send_sem, recv_sem, n, at_src, at_dst, src, dst, peer):
        return pltpu.make_async_remote_copy(
            src_ref=src,
            dst_ref=dst,
            send_sem=send_sem.at[n, at_src],
            recv_sem=recv_sem.at[n, at_dst],
            device_id=peer,
            device_id_type=MESH,
        )

    def q_sum(n, g, r_q, s_q):
        for k in range(1, 8):
            to = (q + k) % 8
            c = copy(rs_send, rs_recv, n, to, q, g.at[:, :, to], r_q.at[q], q_peer(k))
            c.start()
            sends.append(c)
        total = g[:, :, q].astype(F32)
        for k in range(1, 8):
            at = (q + k) % 8
            copy(
                rs_send, rs_recv, n, at, at, g.at[:, :, at], r_q.at[at], q_peer(k)
            ).wait_recv()
            total = total + r_q[at].astype(F32)
        s_q[...] = total.astype(BF16)

    def last_copy(u, g, h, k, src):
        to = ring(x, k)
        return pltpu.make_async_remote_copy(
            src_ref=src.at[to],
            dst_ref=r_last.at[g, zh * 4 + x],
            send_sem=last_send.at[u, to],
            recv_sem=last_recv.at[g, zh * 4 + x],
            device_id=(b, h * 32 + to * 8 + q),
            device_id_type=MESH,
        )

    def last_start(*which):
        for k in range(1, 4):
            last_copy(*which[:3], k, which[3]).start()

        @pl.when(zh != which[2])
        def _():
            last_copy(*which[:3], 0, which[3]).start()

        @pl.when(zh == which[2])
        def _():
            r_last[which[1], zh * 4 + x] = which[3][x]

    def last_drain(*which):
        for k in range(1, 4):
            last_copy(*which[:3], k, which[3]).wait_send()

        @pl.when(zh != which[2])
        def _():
            last_copy(*which[:3], 0, which[3]).wait_send()

    def finish(g, out_ref):
        for k in range(1, 8):
            at = (zh * 4 + x + k) % 8
            pltpu.make_async_remote_copy(
                src_ref=r_last.at[g, at],
                dst_ref=r_last.at[g, at],
                send_sem=last_send.at[g, 0],
                recv_sem=last_recv.at[g, at],
                device_id=zh_peer,
                device_id_type=MESH,
            ).wait_recv()
        total = r_last[g, 0].astype(F32)
        for at in range(1, 8):
            total = total + r_last[g, at].astype(F32)
        for a in range(NBL):
            out_ref[a] = total[2 * a : 2 * a + 2]

    def second(sources, h, store):
        for s in sources:
            act_copy(s, s).wait_recv()
        rows = pl.ds(pl.multiple_of(h * 64, 64), 64)
        for d in range(NBL):
            cols = slice(d * BS, (d + 1) * BS)
            part[d, :64] = dot_nn(recv_act[d, rows, :], og_ref[:, cols]).astype(BF16)
        for s in range(4):
            store[s] = swapped(part, s).reshape(8, 16, BS)

    for a in range(NBL):
        cols = slice(a * BS, (a + 1) * BS)
        pg = (recv_mg[a].astype(F32) * dgelu[a]).astype(BF16)
        tmp[a] = pg
        grad = dot_nn(pg, x_ref[:, cols]).astype(BF16)
        part[a] = dot_tn(grad, placing).astype(BF16)
    for s in range(NBL):
        g_early[s // 4, s % 4] = swapped(part, s).reshape(8, 16, BS)
    second(near, half, g_early.at[2])
    q_sum(0, g_early, rq_early, sq_early)
    lasts = [
        (0, 0, 0, sq_early.at[0]),
        (1, 0, 1, sq_early.at[1]),
        (2, 1, half, sq_early.at[2]),
        (3, 1, 1 - half, sq_late.at[0]),
    ]
    for last in lasts[:3]:
        last_start(*last)

    for a in range(NBL):
        cols = slice(a * BS, (a + 1) * BS)
        ig_ref[:, cols] = dot_tn(tmp[a], wm[a]).astype(BF16)

    second(far, 1 - half, g_late.at[0])
    q_sum(1, g_late, rq_late, sq_late)
    last_start(*lasts[3])

    finish(0, fg_ref)
    finish(1, lg_ref)
    for s in others:
        mg_copy(s, b).wait_send()
        act_copy(s, b).wait_send()
    for c in sends:
        c.wait_send()
    for last in lasts:
        last_drain(*last)


def publish(fg_in, lg_in, ig_in, fg_out, lg_out, ig_out, sem):
    copies = [
        pltpu.make_async_copy(src, dst, sem.at[i])
        for i, (src, dst) in enumerate(((ig_in, ig_out), (fg_in, fg_out), (lg_in, lg_out)))
    ]
    for copy in copies:
        copy.start()
    for copy in copies:
        copy.wait()


def per_device(tokens, first_blocks, latter_factor_blocks, block_perm, out_grad):
    vmem = pl.BlockSpec(memory_space=pltpu.VMEM)
    hbm = pl.BlockSpec(memory_space=pltpu.HBM)
    tokens, first_blocks, latter_factor_blocks, block_perm, out_grad = [pltpu.with_memory_space_constraint(v, pltpu.HBM) for v in (tokens, first_blocks, latter_factor_blocks, block_perm.reshape(1, 64), out_grad)]
    outs = pl.pallas_call(
        kernel,
        out_shape=(
            jax.ShapeDtypeStruct((NBL, 2, BS), F32),
            jax.ShapeDtypeStruct((NBL, 2, BS), F32),
            jax.ShapeDtypeStruct((ROWS, NBL * BS), BF16),
        ),
        in_specs=[hbm] * 5,
        out_specs=[vmem] * 3,
        scratch_shapes=[
            pltpu.VMEM((ROWS, NBL * BS), BF16),
            pltpu.VMEM((NBL, BS, BS), BF16),
            pltpu.VMEM((NBL, BS, BS), BF16),
            pltpu.VMEM((1, 64), jnp.int32),
            pltpu.VMEM((ROWS, NBL * BS), BF16),
            pltpu.SemaphoreType.DMA((5,)),
            pltpu.VMEM((NBL, BS, BS), BF16),
            pltpu.VMEM((NBL, BS, ROWS), BF16),
            pltpu.VMEM((NBL, BS, ROWS), BF16),
            pltpu.VMEM((NBL, BS, ROWS), F32),
            pltpu.VMEM((NBL, NBL, 16, ROWS), BF16),
            pltpu.VMEM((NBL, BS, ROWS), BF16),
            pltpu.VMEM((NBL, NBL, 16, ROWS), BF16),
            pltpu.VMEM((NBL, BS, ROWS), BF16),
            pltpu.VMEM((NBL, BS, BS), BF16),
            pltpu.VMEM((3, 4, 8, 16, BS), BF16),
            pltpu.VMEM((8, 3, 4, 16, BS), BF16),
            pltpu.VMEM((3, 4, 16, BS), BF16),
            pltpu.VMEM((1, 4, 8, 16, BS), BF16),
            pltpu.VMEM((8, 1, 4, 16, BS), BF16),
            pltpu.VMEM((1, 4, 16, BS), BF16),
            pltpu.VMEM((2, 8, 16, BS), BF16),
            pltpu.SemaphoreType.DMA((2, NBL)),
            pltpu.SemaphoreType.DMA((2, NBL)),
            pltpu.SemaphoreType.DMA((2, 8)),
            pltpu.SemaphoreType.DMA((2, 8)),
            pltpu.SemaphoreType.DMA((4, 4)),
            pltpu.SemaphoreType.DMA((2, 8)),
            pltpu.SemaphoreType.REGULAR,
            pltpu.SemaphoreType.REGULAR,
            pltpu.SemaphoreType.REGULAR,
            pltpu.SemaphoreType.REGULAR((8,)),
            pltpu.SemaphoreType.REGULAR((8,)),
        ],
        compiler_params=pltpu.CompilerParams(
            collective_id=0, has_side_effects=True, vmem_limit_bytes=24 * 2**20
        ),
    )(tokens, first_blocks, latter_factor_blocks, block_perm, out_grad)
    return pl.pallas_call(
        publish,
        out_shape=tuple(jax.ShapeDtypeStruct(o.shape, o.dtype) for o in outs),
        in_specs=[vmem] * 3,
        out_specs=[hbm] * 3,
        scratch_shapes=[pltpu.SemaphoreType.DMA((3,))],
        compiler_params=pltpu.CompilerParams(vmem_limit_bytes=16 * 2**20),
    )(*outs)


def solution(mesh):
    return jax.shard_map(
        per_device,
        mesh=mesh,
        in_specs=(
            P("tok", "blk"),
            P("blk", None, None),
            P("blk", None, None),
            P(),
            P("tok", "blk"),
        ),
        out_specs=(P("blk", "tok", None), P("blk", "tok", None), P("tok", "blk")),
        check_vma=False,
    )
```

```python
import jax
import jax.numpy as jnp
from jax import lax
from jax.experimental import pallas as pl
from jax.experimental.pallas import tpu as pltpu
from jax.sharding import PartitionSpec as P

MESH = pl.DeviceIdType.MESH
F32 = jnp.float32
BF16 = jnp.bfloat16
ROWS = 256
BS = 128
NBL = 8


def dot_nn(a, b):
    return lax.dot_general(a, b, (((1,), (0,)), ((), ())), preferred_element_type=F32)


def dot_nt(a, b):
    return lax.dot_general(a, b, (((1,), (1,)), ((), ())), preferred_element_type=F32)


def dot_tn(a, b):
    return lax.dot_general(a, b, (((0,), (0,)), ((), ())), preferred_element_type=F32)


def iota(dim):
    return lax.broadcasted_iota(jnp.int32, (BS, BS), dim)


def one_hot(hit):
    return jnp.where(hit, 1.0, 0.0).astype(BF16)


def kernel(
    x_hbm, w_hbm, l_hbm, perm_hbm, og_hbm,
    fg_ref, lg_ref, ig_ref,
    x_ref, w_ref, l_ref, perm_ref, og_ref, in_sem,
    wm, tmp, act, dgelu, send_mg, recv_mg, send_act, recv_act, part,
    g_early, rq_early, sq_early, g_late, rq_late, sq_late, r_last, r_x, s_x, r_across,
    a2a_send, a2a_recv, rs_send, rs_recv, last_send, last_recv, x_send, x_recv, across_send, across_recv, edge_sem, edge_x_sem, open_sem, up_sem, down_sem,
):
    b = lax.axis_index("blk")
    t = lax.axis_index("tok")
    zh, x, q = t // 32, (t // 8) % 4, t % 8
    half, place = b // 4, b % 4

    def ring(at, k):
        return (at + k) % 4

    zh_peer = (b, t + 32 - 64 * zh)

    def q_peer(k):
        return (b, t + (q + k) % 8 - q)

    def x_peer(k):
        return (b, t + (ring(x, k) - x) * 8)

    far = [half * (3 - k) + (1 - half) * (4 + k) for k in range(4)]
    near = [half * 4 + ring(place, k) for k in range(1, 4)]
    others = far + near
    inner = half * place + (1 - half) * (3 - place)

    at_edge = b == 7 - 7 * zh
    edge_peer = (7 - b, t + 32 - 64 * zh)

    def signal(sem, peer):
        pl.semaphore_signal(sem, inc=1, device_id=peer, device_id_type=MESH)

    barrier = pltpu.get_barrier_semaphore()
    plane = [q_peer(k) for k in range(1, 8)] + [x_peer(k) for k in range(1, 4)]

    @pl.when(b > 0)
    def _():
        signal(barrier, (b - 1, t))

    @pl.when(b < 7)
    def _():
        signal(barrier, (b + 1, t))

    @pl.when(at_edge)
    def _():
        for peer in [*plane, edge_peer]:
            signal(barrier, peer)

    loads = [
        pltpu.make_async_copy(src, dst, in_sem.at[i])
        for i, (src, dst) in enumerate(
            (
                (og_hbm, og_ref),
                (l_hbm, l_ref),
                (w_hbm, w_ref),
                (x_hbm, x_ref),
                (perm_hbm, perm_ref),
            )
        )
    ]
    for load in loads:
        load.start()

    row, col = iota(0), iota(1)
    swap = one_hot(col == ((row >> 1) & 7) * 16 + (row >> 4) * 2 + (row & 1))

    def slab(s):
        return pl.ds(pl.multiple_of(s * 16, 16), 16)

    def a2a(phase, to, at, send, recv):
        return pltpu.make_async_remote_copy(
            src_ref=send.at[to],
            dst_ref=recv.at[:, slab(at), :],
            send_sem=a2a_send.at[phase, to],
            recv_sem=a2a_recv.at[phase, at],
            device_id=(to, t),
            device_id_type=MESH,
        )

    def mg_copy(to, at):
        return a2a(0, to, at, send_mg, recv_mg)

    def act_copy(to, at):
        return a2a(1, to, at, send_act, recv_act)

    def swapped(src, s):
        width = src.shape[-1]
        chunk = src[:, slab(s), :].reshape(BS, width)
        return dot_nn(swap, chunk).astype(BF16).reshape(NBL, 16, width)

    loads[0].wait()
    loads[1].wait()
    for d in range(NBL):
        cols = slice(d * BS, (d + 1) * BS)
        tmp[d] = dot_nt(l_ref[d], og_ref[:, cols]).astype(BF16)

    def entered(k):
        up, down = b + k, b - k

        @pl.when(down >= 0)
        def _():
            if k > 1:
                pl.semaphore_wait(down_sem.at[k], 1)
            if k < 7:

                @pl.when(b < 7)
                def _():
                    signal(down_sem.at[k + 1], (b + 1, t))

            send_mg[down] = swapped(tmp, down)
            mg_copy(down, b).start()

        @pl.when(up < 8)
        def _():
            if k > 1:
                pl.semaphore_wait(up_sem.at[k], 1)
            if k < 7:

                @pl.when(b > 0)
                def _():
                    signal(up_sem.at[k + 1], (b - 1, t))

            send_mg[up] = swapped(tmp, up)
            mg_copy(up, b).start()

    def activation(a):
        cols = slice(a * BS, (a + 1) * BS)
        wm[a] = dot_nt(placing, w_ref[a]).astype(BF16)
        pre = dot_nt(wm[a], x_ref[:, cols])
        cdf = 0.5 * (1.0 + lax.erf(pre * 0.7071067811865476))
        act[a] = (pre * cdf).astype(BF16)
        dgelu[a] = cdf + pre * 0.3989422804014327 * jnp.exp(-0.5 * pre * pre)

    pl.semaphore_wait(
        barrier,
        jnp.where(b > 0, 1, 0) + jnp.where(b < 7, 1, 0) + jnp.where(at_edge, 11, 0),
    )
    entered(1)
    for load in loads[2:]:
        load.wait()
    perm = jnp.broadcast_to(perm_ref[...].astype(F32), (16, 64)).astype(BF16)
    pair = one_hot(iota(1)[:64] // 2 == iota(0)[:64])
    target = dot_nn(perm, pair)[:1] * 2.0 + (iota(1)[:1] % 2).astype(F32)
    placing = one_hot(iota(0).astype(F32) == target)
    for k in range(2, 6):
        activation(2 * k - 4)
        activation(2 * k - 3)
        entered(k)
    entered(6)
    entered(7)
    recv_mg[:, slab(b), :] = swapped(tmp, b)

    @pl.when(at_edge)
    def _():
        for peer in [*plane, edge_peer]:
            signal(edge_sem, peer)

    for s in near:
        send_act[s] = swapped(act, s)
        act_copy(s, b).start()
    for s in far:
        send_act[s] = swapped(act, s)
    recv_act[:, slab(b), :] = swapped(act, b)

    @pl.when(jnp.logical_not(inner >= 3))
    def _():
        for s in far:
            act_copy(s, b).start()

    @pl.when(at_edge)
    def _():
        pl.semaphore_wait(edge_sem, 11)
        for k in range(1, 4):
            signal(edge_x_sem, x_peer(k))
        pl.semaphore_wait(edge_x_sem, 3)
        for k in range(1, 8):
            signal(open_sem, ((b + k) % 8, t))

    @pl.when(jnp.logical_not(at_edge))
    def _():
        pl.semaphore_wait(open_sem, 1)

    for s in others:
        mg_copy(s, s).wait_recv()

    @pl.when(inner >= 3)
    def _():
        for s in far:
            act_copy(s, b).start()

    sends = []

    def copy(send_sem, recv_sem, n, at_src, at_dst, src, dst, peer):
        return pltpu.make_async_remote_copy(
            src_ref=src,
            dst_ref=dst,
            send_sem=send_sem.at[n, at_src],
            recv_sem=recv_sem.at[n, at_dst],
            device_id=peer,
            device_id_type=MESH,
        )

    def q_sum(n, g, r_q, s_q):
        for k in range(1, 8):
            to = (q + k) % 8
            c = copy(rs_send, rs_recv, n, to, q, g.at[:, :, to], r_q.at[q], q_peer(k))
            c.start()
            sends.append(c)
        total = g[:, :, q].astype(F32)
        for k in range(1, 8):
            at = (q + k) % 8
            copy(
                rs_send, rs_recv, n, at, at, g.at[:, :, at], r_q.at[at], q_peer(k)
            ).wait_recv()
            total = total + r_q[at].astype(F32)
        s_q[...] = total.astype(BF16)

    def last_copy(u, g, h, k, src):
        to = ring(x, k)
        return pltpu.make_async_remote_copy(
            src_ref=src.at[to],
            dst_ref=r_last.at[g, zh * 4 + x],
            send_sem=last_send.at[u, to],
            recv_sem=last_recv.at[g, zh * 4 + x],
            device_id=(b, h * 32 + to * 8 + q),
            device_id_type=MESH,
        )

    def last_start(*which):
        for k in range(1, 4):
            last_copy(*which[:3], k, which[3]).start()

        @pl.when(zh != which[2])
        def _():
            last_copy(*which[:3], 0, which[3]).start()

        @pl.when(zh == which[2])
        def _():
            r_last[which[1], zh * 4 + x] = which[3][x]

    def last_drain(*which):
        for k in range(1, 4):
            last_copy(*which[:3], k, which[3]).wait_send()

        @pl.when(zh != which[2])
        def _():
            last_copy(*which[:3], 0, which[3]).wait_send()

    def across(g, src):
        return pltpu.make_async_remote_copy(
            src_ref=src,
            dst_ref=r_across.at[g],
            send_sem=across_send.at[g],
            recv_sem=across_recv.at[g],
            device_id=zh_peer,
            device_id_type=MESH,
        )

    def early_copy(to, at, k):
        return pltpu.make_async_remote_copy(
            src_ref=sq_early.at[:, to],
            dst_ref=r_x.at[at],
            send_sem=x_send.at[to],
            recv_sem=x_recv.at[at],
            device_id=x_peer(k),
            device_id_type=MESH,
        )

    def put(total, out_ref):
        for a in range(NBL):
            out_ref[a] = total[2 * a : 2 * a + 2]

    def second(sources, h, store):
        for s in sources:
            act_copy(s, s).wait_recv()
        rows = pl.ds(pl.multiple_of(h * 64, 64), 64)
        for d in range(NBL):
            cols = slice(d * BS, (d + 1) * BS)
            part[d, :64] = dot_nn(recv_act[d, rows, :], og_ref[:, cols]).astype(BF16)
        for s in range(4):
            store[s] = swapped(part, s).reshape(8, 16, BS)

    for a in range(NBL):
        cols = slice(a * BS, (a + 1) * BS)
        pg = (recv_mg[a].astype(F32) * dgelu[a]).astype(BF16)
        tmp[a] = pg
        grad = dot_nn(pg, x_ref[:, cols]).astype(BF16)
        part[a] = dot_tn(grad, placing).astype(BF16)
    for s in range(NBL):
        g_early[s // 4, s % 4] = swapped(part, s).reshape(8, 16, BS)
    second(near, half, g_early.at[2])
    q_sum(0, g_early, rq_early, sq_early)
    for k in range(1, 4):
        early_copy(ring(x, k), x, k).start()
    total = sq_early[:, x].astype(F32)
    for k in range(1, 4):
        at = ring(x, k)
        early_copy(at, at, k).wait_recv()
        total = total + r_x[at].astype(F32)
    s_x[...] = total.astype(BF16)
    across(0, s_x.at[1 - zh]).start()

    @pl.when(zh != half)
    def _():
        across(1, s_x.at[2]).start()

    for a in range(NBL):
        cols = slice(a * BS, (a + 1) * BS)
        ig_ref[:, cols] = dot_tn(tmp[a], wm[a]).astype(BF16)

    second(far, 1 - half, g_late.at[0])
    q_sum(1, g_late, rq_late, sq_late)
    last = (0, 0, 1 - half, sq_late.at[0])
    last_start(*last)

    across(0, s_x.at[1 - zh]).wait_recv()
    put(s_x[zh].astype(F32) + r_across[0].astype(F32), fg_ref)

    @pl.when(zh == half)
    def _():
        across(1, s_x.at[2]).wait_recv()
        put(s_x[2].astype(F32) + r_across[1].astype(F32), lg_ref)

    @pl.when(zh != half)
    def _():
        for k in range(1, 8):
            at = (zh * 4 + x + k) % 8
            pltpu.make_async_remote_copy(
                src_ref=r_last.at[0, at],
                dst_ref=r_last.at[0, at],
                send_sem=last_send.at[0, 0],
                recv_sem=last_recv.at[0, at],
                device_id=zh_peer,
                device_id_type=MESH,
            ).wait_recv()
        total = r_last[0, 0].astype(F32)
        for at in range(1, 8):
            total = total + r_last[0, at].astype(F32)
        put(total, lg_ref)

    for s in others:
        mg_copy(s, b).wait_send()
        act_copy(s, b).wait_send()
    for c in sends:
        c.wait_send()
    last_drain(*last)
    for k in range(1, 4):
        early_copy(ring(x, k), x, k).wait_send()
    across(0, s_x.at[1 - zh]).wait_send()

    @pl.when(zh != half)
    def _():
        across(1, s_x.at[2]).wait_send()


def publish(fg_in, lg_in, ig_in, fg_out, lg_out, ig_out, sem):
    copies = [
        pltpu.make_async_copy(src, dst, sem.at[i])
        for i, (src, dst) in enumerate(((ig_in, ig_out), (fg_in, fg_out), (lg_in, lg_out)))
    ]
    for copy in copies:
        copy.start()
    for copy in copies:
        copy.wait()


def per_device(tokens, first_blocks, latter_factor_blocks, block_perm, out_grad):
    vmem = pl.BlockSpec(memory_space=pltpu.VMEM)
    hbm = pl.BlockSpec(memory_space=pltpu.HBM)
    tokens, first_blocks, latter_factor_blocks, block_perm, out_grad = [pltpu.with_memory_space_constraint(v, pltpu.HBM) for v in (tokens, first_blocks, latter_factor_blocks, block_perm.reshape(1, 64), out_grad)]
    outs = pl.pallas_call(
        kernel,
        out_shape=(
            jax.ShapeDtypeStruct((NBL, 2, BS), F32),
            jax.ShapeDtypeStruct((NBL, 2, BS), F32),
            jax.ShapeDtypeStruct((ROWS, NBL * BS), BF16),
        ),
        in_specs=[hbm] * 5,
        out_specs=[vmem] * 3,
        scratch_shapes=[
            pltpu.VMEM((ROWS, NBL * BS), BF16),
            pltpu.VMEM((NBL, BS, BS), BF16),
            pltpu.VMEM((NBL, BS, BS), BF16),
            pltpu.VMEM((1, 64), jnp.int32),
            pltpu.VMEM((ROWS, NBL * BS), BF16),
            pltpu.SemaphoreType.DMA((5,)),
            pltpu.VMEM((NBL, BS, BS), BF16),
            pltpu.VMEM((NBL, BS, ROWS), BF16),
            pltpu.VMEM((NBL, BS, ROWS), BF16),
            pltpu.VMEM((NBL, BS, ROWS), F32),
            pltpu.VMEM((NBL, NBL, 16, ROWS), BF16),
            pltpu.VMEM((NBL, BS, ROWS), BF16),
            pltpu.VMEM((NBL, NBL, 16, ROWS), BF16),
            pltpu.VMEM((NBL, BS, ROWS), BF16),
            pltpu.VMEM((NBL, BS, BS), BF16),
            pltpu.VMEM((3, 4, 8, 16, BS), BF16),
            pltpu.VMEM((8, 3, 4, 16, BS), BF16),
            pltpu.VMEM((3, 4, 16, BS), BF16),
            pltpu.VMEM((1, 4, 8, 16, BS), BF16),
            pltpu.VMEM((8, 1, 4, 16, BS), BF16),
            pltpu.VMEM((1, 4, 16, BS), BF16),
            pltpu.VMEM((1, 8, 16, BS), BF16),
            pltpu.VMEM((4, 3, 16, BS), BF16),
            pltpu.VMEM((3, 16, BS), BF16),
            pltpu.VMEM((2, 16, BS), BF16),
            pltpu.SemaphoreType.DMA((2, NBL)),
            pltpu.SemaphoreType.DMA((2, NBL)),
            pltpu.SemaphoreType.DMA((2, 8)),
            pltpu.SemaphoreType.DMA((2, 8)),
            pltpu.SemaphoreType.DMA((1, 4)),
            pltpu.SemaphoreType.DMA((1, 8)),
            pltpu.SemaphoreType.DMA((4,)),
            pltpu.SemaphoreType.DMA((4,)),
            pltpu.SemaphoreType.DMA((2,)),
            pltpu.SemaphoreType.DMA((2,)),
            pltpu.SemaphoreType.REGULAR,
            pltpu.SemaphoreType.REGULAR,
            pltpu.SemaphoreType.REGULAR,
            pltpu.SemaphoreType.REGULAR((8,)),
            pltpu.SemaphoreType.REGULAR((8,)),
        ],
        compiler_params=pltpu.CompilerParams(
            collective_id=0, has_side_effects=True, vmem_limit_bytes=24 * 2**20
        ),
    )(tokens, first_blocks, latter_factor_blocks, block_perm, out_grad)
    return pl.pallas_call(
        publish,
        out_shape=tuple(jax.ShapeDtypeStruct(o.shape, o.dtype) for o in outs),
        in_specs=[vmem] * 3,
        out_specs=[hbm] * 3,
        scratch_shapes=[pltpu.SemaphoreType.DMA((3,))],
        compiler_params=pltpu.CompilerParams(vmem_limit_bytes=16 * 2**20),
    )(*outs)


def solution(mesh):
    return jax.shard_map(
        per_device,
        mesh=mesh,
        in_specs=(
            P("tok", "blk"),
            P("blk", None, None),
            P("blk", None, None),
            P(),
            P("tok", "blk"),
        ),
        out_specs=(P("blk", "tok", None), P("blk", "tok", None), P("tok", "blk")),
        check_vma=False,
    )
```

```python
import jax
import jax.numpy as jnp
from jax import lax
from jax.experimental import pallas as pl
from jax.experimental.pallas import tpu as pltpu
from jax.sharding import PartitionSpec as P

MESH = pl.DeviceIdType.MESH
F32 = jnp.float32
BF16 = jnp.bfloat16
ROWS = 256
BS = 128
NBL = 8


def dot_nn(a, b):
    return lax.dot_general(a, b, (((1,), (0,)), ((), ())), preferred_element_type=F32)


def dot_nt(a, b):
    return lax.dot_general(a, b, (((1,), (1,)), ((), ())), preferred_element_type=F32)


def dot_tn(a, b):
    return lax.dot_general(a, b, (((0,), (0,)), ((), ())), preferred_element_type=F32)


def iota(dim):
    return lax.broadcasted_iota(jnp.int32, (BS, BS), dim)


def one_hot(hit):
    return jnp.where(hit, 1.0, 0.0).astype(BF16)


def kernel(
    x_hbm, w_hbm, l_hbm, perm_hbm, og_hbm,
    fg_ref, lg_ref, ig_ref,
    x_ref, w_ref, l_ref, perm_ref, og_ref, in_sem,
    wm, tmp, act, dgelu, send_mg, recv_mg, send_act, recv_act, part,
    g_early, rq_early, sq_early, g_late, rq_late, sq_late, r_last, r_x, s_x, r_across,
    a2a_send, a2a_recv, rs_send, rs_recv, last_send, last_recv, x_send, x_recv, across_send, across_recv, edge_sem, edge_x_sem, open_sem, up_sem, down_sem,
):
    b = lax.axis_index("blk")
    t = lax.axis_index("tok")
    zh, x, q = t // 32, (t // 8) % 4, t % 8
    half, place = b // 4, b % 4

    def ring(at, k):
        return (at + k) % 4

    zh_peer = (b, t + 32 - 64 * zh)

    def q_peer(k):
        return (b, t + (q + k) % 8 - q)

    def x_peer(k):
        return (b, t + (ring(x, k) - x) * 8)

    far = [half * (3 - k) + (1 - half) * (4 + k) for k in range(4)]
    near = [half * 4 + ring(place, k) for k in range(1, 4)]
    others = far + near
    inner = half * place + (1 - half) * (3 - place)

    at_edge = b == 7 - 7 * zh
    edge_peer = (7 - b, t + 32 - 64 * zh)

    def signal(sem, peer):
        pl.semaphore_signal(sem, inc=1, device_id=peer, device_id_type=MESH)

    barrier = pltpu.get_barrier_semaphore()
    plane = [q_peer(k) for k in range(1, 8)] + [x_peer(k) for k in range(1, 4)]

    @pl.when(b > 0)
    def _():
        signal(barrier, (b - 1, t))

    @pl.when(b < 7)
    def _():
        signal(barrier, (b + 1, t))

    @pl.when(at_edge)
    def _():
        for peer in [*plane, edge_peer]:
            signal(barrier, peer)

    loads = [
        pltpu.make_async_copy(src, dst, in_sem.at[i])
        for i, (src, dst) in enumerate(
            (
                (og_hbm, og_ref),
                (l_hbm, l_ref),
                (w_hbm, w_ref),
                (x_hbm, x_ref),
                (perm_hbm, perm_ref),
            )
        )
    ]
    for load in loads:
        load.start()

    row, col = iota(0), iota(1)
    swap = one_hot(col == ((row >> 1) & 7) * 16 + (row >> 4) * 2 + (row & 1))

    def slab(s):
        return pl.ds(pl.multiple_of(s * 16, 16), 16)

    def a2a(phase, to, at, send, recv):
        return pltpu.make_async_remote_copy(
            src_ref=send.at[to],
            dst_ref=recv.at[:, slab(at), :],
            send_sem=a2a_send.at[phase, to],
            recv_sem=a2a_recv.at[phase, at],
            device_id=(to, t),
            device_id_type=MESH,
        )

    def mg_copy(to, at):
        return a2a(0, to, at, send_mg, recv_mg)

    def act_copy(to, at):
        return a2a(1, to, at, send_act, recv_act)

    def swapped(src, s):
        width = src.shape[-1]
        chunk = src[:, slab(s), :].reshape(BS, width)
        return dot_nn(swap, chunk).astype(BF16).reshape(NBL, 16, width)

    loads[0].wait()
    loads[1].wait()
    for d in range(NBL):
        cols = slice(d * BS, (d + 1) * BS)
        tmp[d] = dot_nt(l_ref[d], og_ref[:, cols]).astype(BF16)

    def entered(k):
        up, down = b + k, b - k

        @pl.when(down >= 0)
        def _():
            if k > 1:
                pl.semaphore_wait(down_sem.at[k], 1)
            if k < 7:

                @pl.when(b < 7)
                def _():
                    signal(down_sem.at[k + 1], (b + 1, t))

            send_mg[down] = swapped(tmp, down)
            mg_copy(down, b).start()

        @pl.when(up < 8)
        def _():
            if k > 1:
                pl.semaphore_wait(up_sem.at[k], 1)
            if k < 7:

                @pl.when(b > 0)
                def _():
                    signal(up_sem.at[k + 1], (b - 1, t))

            send_mg[up] = swapped(tmp, up)
            mg_copy(up, b).start()

    def activation(a):
        cols = slice(a * BS, (a + 1) * BS)
        wm[a] = dot_nt(placing, w_ref[a]).astype(BF16)
        pre = dot_nt(wm[a], x_ref[:, cols])
        cdf = 0.5 * (1.0 + lax.erf(pre * 0.7071067811865476))
        act[a] = (pre * cdf).astype(BF16)
        dgelu[a] = cdf + pre * 0.3989422804014327 * jnp.exp(-0.5 * pre * pre)

    pl.semaphore_wait(
        barrier,
        jnp.where(b > 0, 1, 0) + jnp.where(b < 7, 1, 0) + jnp.where(at_edge, 11, 0),
    )
    entered(1)
    for load in loads[2:]:
        load.wait()
    perm = jnp.broadcast_to(perm_ref[...].astype(F32), (16, 64)).astype(BF16)
    pair = one_hot(iota(1)[:64] // 2 == iota(0)[:64])
    target = dot_nn(perm, pair)[:1] * 2.0 + (iota(1)[:1] % 2).astype(F32)
    placing = one_hot(iota(0).astype(F32) == target)
    for k in range(2, 6):
        activation(2 * k - 4)
        activation(2 * k - 3)
        entered(k)
    entered(6)
    entered(7)
    recv_mg[:, slab(b), :] = swapped(tmp, b)

    @pl.when(at_edge)
    def _():
        for peer in [*plane, edge_peer]:
            signal(edge_sem, peer)

    for s in near:
        send_act[s] = swapped(act, s)
        act_copy(s, b).start()
    for s in far:
        send_act[s] = swapped(act, s)
    recv_act[:, slab(b), :] = swapped(act, b)

    @pl.when(jnp.logical_not(inner >= 3))
    def _():
        for s in far:
            act_copy(s, b).start()

    @pl.when(at_edge)
    def _():
        pl.semaphore_wait(edge_sem, 11)
        for k in range(1, 4):
            signal(edge_x_sem, x_peer(k))
        pl.semaphore_wait(edge_x_sem, 3)
        for k in range(1, 8):
            signal(open_sem, ((b + k) % 8, t))

    @pl.when(jnp.logical_not(at_edge))
    def _():
        pl.semaphore_wait(open_sem, 1)

    for s in others:
        mg_copy(s, s).wait_recv()

    @pl.when(inner >= 3)
    def _():
        for s in far:
            act_copy(s, b).start()

    sends = []

    def copy(send_sem, recv_sem, n, at_src, at_dst, src, dst, peer):
        return pltpu.make_async_remote_copy(
            src_ref=src,
            dst_ref=dst,
            send_sem=send_sem.at[n, at_src],
            recv_sem=recv_sem.at[n, at_dst],
            device_id=peer,
            device_id_type=MESH,
        )

    def q_sum(n, src, land):
        for k in range(1, 8):
            to = (q + k) % 8
            c = copy(rs_send, rs_recv, n, to, q, src(to), land(q), q_peer(k))
            c.start()
            sends.append(c)
        total = src(q)[...].astype(F32)
        for k in range(1, 8):
            at = (q + k) % 8
            copy(rs_send, rs_recv, n, at, at, src(at), land(at), q_peer(k)).wait_recv()
            total = total + land(at)[...].astype(F32)
        return total.astype(BF16)

    def last_copy(u, g, h, k, src):
        to = ring(x, k)
        return pltpu.make_async_remote_copy(
            src_ref=src.at[to],
            dst_ref=r_last.at[g, zh * 4 + x],
            send_sem=last_send.at[u, to],
            recv_sem=last_recv.at[g, zh * 4 + x],
            device_id=(b, h * 32 + to * 8 + q),
            device_id_type=MESH,
        )

    def last_start(h, pick):
        for k in range(4):
            goes = pick(ring(x, k))
            if k == 0:
                goes = jnp.logical_and(goes, zh != h)

            @pl.when(goes)
            def _():
                last_copy(0, 0, h, k, sq_late.at[0]).start()

        @pl.when(jnp.logical_and(pick(x), zh == h))
        def _():
            r_last[0, zh * 4 + x] = sq_late[0, x]

    def last_drain(*which):
        for k in range(1, 4):
            last_copy(*which[:3], k, which[3]).wait_send()

        @pl.when(zh != which[2])
        def _():
            last_copy(*which[:3], 0, which[3]).wait_send()

    def across(g, src):
        return pltpu.make_async_remote_copy(
            src_ref=src,
            dst_ref=r_across.at[g],
            send_sem=across_send.at[g],
            recv_sem=across_recv.at[g],
            device_id=zh_peer,
            device_id_type=MESH,
        )

    def early_copy(to, at, k):
        return pltpu.make_async_remote_copy(
            src_ref=sq_early.at[:, to],
            dst_ref=r_x.at[at],
            send_sem=x_send.at[to],
            recv_sem=x_recv.at[at],
            device_id=x_peer(k),
            device_id_type=MESH,
        )

    def put(total, out_ref):
        for a in range(NBL):
            out_ref[a] = total[2 * a : 2 * a + 2]

    def second(at, count, sources, store):
        for s in sources:
            act_copy(s, s).wait_recv()
        rows = pl.ds(pl.multiple_of(at * 16, 16), count * 16)
        for d in range(NBL):
            cols = slice(d * BS, (d + 1) * BS)
            part[d, : count * 16] = dot_nn(
                recv_act[d, rows, :], og_ref[:, cols]
            ).astype(BF16)
        for s in range(count):
            store[at % 4 + s] = swapped(part, s).reshape(8, 16, BS)

    for a in range(NBL):
        cols = slice(a * BS, (a + 1) * BS)
        pg = (recv_mg[a].astype(F32) * dgelu[a]).astype(BF16)
        tmp[a] = pg
        grad = dot_nn(pg, x_ref[:, cols]).astype(BF16)
        part[a] = dot_tn(grad, placing).astype(BF16)
    for s in range(NBL):
        g_early[s // 4, s % 4] = swapped(part, s).reshape(8, 16, BS)
    second(4 * half, 4, near, g_early.at[2])
    sq_early[...] = q_sum(0, lambda to: g_early.at[:, :, to], lambda at: rq_early.at[at])
    for k in range(1, 4):
        early_copy(ring(x, k), x, k).start()
    total = sq_early[:, x].astype(F32)
    for k in range(1, 4):
        at = ring(x, k)
        early_copy(at, at, k).wait_recv()
        total = total + r_x[at].astype(F32)
    s_x[...] = total.astype(BF16)
    across(0, s_x.at[1 - zh]).start()

    @pl.when(zh != half)
    def _():
        across(1, s_x.at[2]).start()

    for a in range(NBL):
        cols = slice(a * BS, (a + 1) * BS)
        ig_ref[:, cols] = dot_tn(tmp[a], wm[a]).astype(BF16)

    inmost = 3 * half
    outer = pl.ds(1 - half, 3)
    second(4 - 4 * half + 1 - half, 3, far[1:], g_late.at[0])
    sq_late[0, outer] = q_sum(
        1, lambda to: g_late.at[0, outer, to], lambda at: rq_late.at[at, 0, outer]
    )
    last_start(1 - half, lambda to: to != inmost)
    second(far[0], 1, far[:1], g_late.at[0])
    sq_late[0, inmost] = q_sum(
        2, lambda to: g_late.at[0, inmost, to], lambda at: rq_late.at[at, 0, inmost]
    )
    last_start(1 - half, lambda to: to == inmost)
    last = (0, 0, 1 - half, sq_late.at[0])

    across(0, s_x.at[1 - zh]).wait_recv()
    put(s_x[zh].astype(F32) + r_across[0].astype(F32), fg_ref)

    @pl.when(zh == half)
    def _():
        across(1, s_x.at[2]).wait_recv()
        put(s_x[2].astype(F32) + r_across[1].astype(F32), lg_ref)

    @pl.when(zh != half)
    def _():
        for k in range(1, 8):
            at = (zh * 4 + x + k) % 8
            pltpu.make_async_remote_copy(
                src_ref=r_last.at[0, at],
                dst_ref=r_last.at[0, at],
                send_sem=last_send.at[0, 0],
                recv_sem=last_recv.at[0, at],
                device_id=zh_peer,
                device_id_type=MESH,
            ).wait_recv()
        total = r_last[0, 0].astype(F32)
        for at in range(1, 8):
            total = total + r_last[0, at].astype(F32)
        put(total, lg_ref)

    for s in others:
        mg_copy(s, b).wait_send()
        act_copy(s, b).wait_send()
    for c in sends:
        c.wait_send()
    last_drain(*last)
    for k in range(1, 4):
        early_copy(ring(x, k), x, k).wait_send()
    across(0, s_x.at[1 - zh]).wait_send()

    @pl.when(zh != half)
    def _():
        across(1, s_x.at[2]).wait_send()


def publish(fg_in, lg_in, ig_in, fg_out, lg_out, ig_out, sem):
    copies = [
        pltpu.make_async_copy(src, dst, sem.at[i])
        for i, (src, dst) in enumerate(((ig_in, ig_out), (fg_in, fg_out), (lg_in, lg_out)))
    ]
    for copy in copies:
        copy.start()
    for copy in copies:
        copy.wait()


def per_device(tokens, first_blocks, latter_factor_blocks, block_perm, out_grad):
    vmem = pl.BlockSpec(memory_space=pltpu.VMEM)
    hbm = pl.BlockSpec(memory_space=pltpu.HBM)
    tokens, first_blocks, latter_factor_blocks, block_perm, out_grad = [pltpu.with_memory_space_constraint(v, pltpu.HBM) for v in (tokens, first_blocks, latter_factor_blocks, block_perm.reshape(1, 64), out_grad)]
    outs = pl.pallas_call(
        kernel,
        out_shape=(
            jax.ShapeDtypeStruct((NBL, 2, BS), F32),
            jax.ShapeDtypeStruct((NBL, 2, BS), F32),
            jax.ShapeDtypeStruct((ROWS, NBL * BS), BF16),
        ),
        in_specs=[hbm] * 5,
        out_specs=[vmem] * 3,
        scratch_shapes=[
            pltpu.VMEM((ROWS, NBL * BS), BF16),
            pltpu.VMEM((NBL, BS, BS), BF16),
            pltpu.VMEM((NBL, BS, BS), BF16),
            pltpu.VMEM((1, 64), jnp.int32),
            pltpu.VMEM((ROWS, NBL * BS), BF16),
            pltpu.SemaphoreType.DMA((5,)),
            pltpu.VMEM((NBL, BS, BS), BF16),
            pltpu.VMEM((NBL, BS, ROWS), BF16),
            pltpu.VMEM((NBL, BS, ROWS), BF16),
            pltpu.VMEM((NBL, BS, ROWS), F32),
            pltpu.VMEM((NBL, NBL, 16, ROWS), BF16),
            pltpu.VMEM((NBL, BS, ROWS), BF16),
            pltpu.VMEM((NBL, NBL, 16, ROWS), BF16),
            pltpu.VMEM((NBL, BS, ROWS), BF16),
            pltpu.VMEM((NBL, BS, BS), BF16),
            pltpu.VMEM((3, 4, 8, 16, BS), BF16),
            pltpu.VMEM((8, 3, 4, 16, BS), BF16),
            pltpu.VMEM((3, 4, 16, BS), BF16),
            pltpu.VMEM((1, 4, 8, 16, BS), BF16),
            pltpu.VMEM((8, 1, 4, 16, BS), BF16),
            pltpu.VMEM((1, 4, 16, BS), BF16),
            pltpu.VMEM((1, 8, 16, BS), BF16),
            pltpu.VMEM((4, 3, 16, BS), BF16),
            pltpu.VMEM((3, 16, BS), BF16),
            pltpu.VMEM((2, 16, BS), BF16),
            pltpu.SemaphoreType.DMA((2, NBL)),
            pltpu.SemaphoreType.DMA((2, NBL)),
            pltpu.SemaphoreType.DMA((3, 8)),
            pltpu.SemaphoreType.DMA((3, 8)),
            pltpu.SemaphoreType.DMA((1, 4)),
            pltpu.SemaphoreType.DMA((1, 8)),
            pltpu.SemaphoreType.DMA((4,)),
            pltpu.SemaphoreType.DMA((4,)),
            pltpu.SemaphoreType.DMA((2,)),
            pltpu.SemaphoreType.DMA((2,)),
            pltpu.SemaphoreType.REGULAR,
            pltpu.SemaphoreType.REGULAR,
            pltpu.SemaphoreType.REGULAR,
            pltpu.SemaphoreType.REGULAR((8,)),
            pltpu.SemaphoreType.REGULAR((8,)),
        ],
        compiler_params=pltpu.CompilerParams(
            collective_id=0, has_side_effects=True, vmem_limit_bytes=24 * 2**20
        ),
    )(tokens, first_blocks, latter_factor_blocks, block_perm, out_grad)
    return pl.pallas_call(
        publish,
        out_shape=tuple(jax.ShapeDtypeStruct(o.shape, o.dtype) for o in outs),
        in_specs=[vmem] * 3,
        out_specs=[hbm] * 3,
        scratch_shapes=[pltpu.SemaphoreType.DMA((3,))],
        compiler_params=pltpu.CompilerParams(vmem_limit_bytes=16 * 2**20),
    )(*outs)


def solution(mesh):
    return jax.shard_map(
        per_device,
        mesh=mesh,
        in_specs=(
            P("tok", "blk"),
            P("blk", None, None),
            P("blk", None, None),
            P(),
            P("tok", "blk"),
        ),
        out_specs=(P("blk", "tok", None), P("blk", "tok", None), P("tok", "blk")),
        check_vma=False,
    )
```

```python
import jax
import jax.numpy as jnp
from jax import lax
from jax.experimental import pallas as pl
from jax.experimental.pallas import tpu as pltpu
from jax.sharding import PartitionSpec as P

MESH = pl.DeviceIdType.MESH
F32 = jnp.float32
BF16 = jnp.bfloat16
ROWS = 256
BS = 128
NBL = 8


def dot_nn(a, b):
    return lax.dot_general(a, b, (((1,), (0,)), ((), ())), preferred_element_type=F32)


def dot_nt(a, b):
    return lax.dot_general(a, b, (((1,), (1,)), ((), ())), preferred_element_type=F32)


def dot_tn(a, b):
    return lax.dot_general(a, b, (((0,), (0,)), ((), ())), preferred_element_type=F32)


def iota(dim):
    return lax.broadcasted_iota(jnp.int32, (BS, BS), dim)


def one_hot(hit):
    return jnp.where(hit, 1.0, 0.0).astype(BF16)


def kernel(
    x_hbm, w_hbm, l_hbm, perm_hbm, og_hbm,
    fg_ref, lg_ref, ig_ref,
    x_ref, w_ref, l_ref, perm_ref, og_ref, in_sem,
    wm, tmp, act, dgelu, send_mg, recv_mg, send_act, recv_act, part,
    g_early, rq_early, sq_early, g_late, rq_late, sq_late, r_last, r_x, s_x, r_across,
    a2a_send, a2a_recv, rs_send, rs_recv, last_send, last_recv, x_send, x_recv, across_send, across_recv, edge_sem, edge_x_sem, open_sem, up_sem, down_sem,
):
    b = lax.axis_index("blk")
    t = lax.axis_index("tok")
    zh, x, q = t // 32, (t // 8) % 4, t % 8
    half, place = b // 4, b % 4

    def ring(at, k):
        return (at + k) % 4

    zh_peer = (b, t + 32 - 64 * zh)

    def q_peer(k):
        return (b, t + (q + k) % 8 - q)

    def x_peer(k):
        return (b, t + (ring(x, k) - x) * 8)

    far = [half * (3 - k) + (1 - half) * (4 + k) for k in range(4)]
    near = [half * 4 + ring(place, k) for k in range(1, 4)]
    others = far + near
    inner = half * place + (1 - half) * (3 - place)

    at_edge = b == 7 - 7 * zh
    edge_peer = (7 - b, t + 32 - 64 * zh)

    def signal(sem, peer):
        pl.semaphore_signal(sem, inc=1, device_id=peer, device_id_type=MESH)

    barrier = pltpu.get_barrier_semaphore()
    plane = [q_peer(k) for k in range(1, 8)] + [x_peer(k) for k in range(1, 4)]

    @pl.when(b > 0)
    def _():
        signal(barrier, (b - 1, t))

    @pl.when(b < 7)
    def _():
        signal(barrier, (b + 1, t))

    @pl.when(at_edge)
    def _():
        for peer in [*plane, edge_peer]:
            signal(barrier, peer)

    loads = [
        pltpu.make_async_copy(src, dst, in_sem.at[i])
        for i, (src, dst) in enumerate(
            (
                (og_hbm, og_ref),
                (l_hbm, l_ref),
                (w_hbm, w_ref),
                (x_hbm, x_ref),
                (perm_hbm, perm_ref),
            )
        )
    ]
    for load in loads:
        load.start()

    row, col = iota(0), iota(1)
    swap = one_hot(col == ((row >> 1) & 7) * 16 + (row >> 4) * 2 + (row & 1))

    def slab(s):
        return pl.ds(pl.multiple_of(s * 16, 16), 16)

    def a2a(phase, to, at, send, recv):
        return pltpu.make_async_remote_copy(
            src_ref=send.at[to],
            dst_ref=recv.at[:, slab(at), :],
            send_sem=a2a_send.at[phase, to],
            recv_sem=a2a_recv.at[phase, at],
            device_id=(to, t),
            device_id_type=MESH,
        )

    def mg_copy(to, at):
        return a2a(0, to, at, send_mg, recv_mg)

    def act_copy(to, at):
        return a2a(1, to, at, send_act, recv_act)

    def swapped(src, s):
        width = src.shape[-1]
        chunk = src[:, slab(s), :].reshape(BS, width)
        return dot_nn(swap, chunk).astype(BF16).reshape(NBL, 16, width)

    loads[0].wait()
    loads[1].wait()
    for d in range(NBL):
        cols = slice(d * BS, (d + 1) * BS)
        tmp[d] = dot_nt(l_ref[d], og_ref[:, cols]).astype(BF16)

    def entered(k):
        up, down = b + k, b - k

        @pl.when(down >= 0)
        def _():
            if k > 1:
                pl.semaphore_wait(down_sem.at[k], 1)
            if k < 7:

                @pl.when(b < 7)
                def _():
                    signal(down_sem.at[k + 1], (b + 1, t))

            send_mg[down] = swapped(tmp, down)
            mg_copy(down, b).start()

        @pl.when(up < 8)
        def _():
            if k > 1:
                pl.semaphore_wait(up_sem.at[k], 1)
            if k < 7:

                @pl.when(b > 0)
                def _():
                    signal(up_sem.at[k + 1], (b - 1, t))

            send_mg[up] = swapped(tmp, up)
            mg_copy(up, b).start()

    def activation(a):
        cols = slice(a * BS, (a + 1) * BS)
        wm[a] = dot_nt(placing, w_ref[a]).astype(BF16)
        pre = dot_nt(wm[a], x_ref[:, cols])
        cdf = 0.5 * (1.0 + lax.erf(pre * 0.7071067811865476))
        act[a] = (pre * cdf).astype(BF16)
        dgelu[a] = cdf + pre * 0.3989422804014327 * jnp.exp(-0.5 * pre * pre)

    pl.semaphore_wait(
        barrier,
        jnp.where(b > 0, 1, 0) + jnp.where(b < 7, 1, 0) + jnp.where(at_edge, 11, 0),
    )
    entered(1)
    for load in loads[2:]:
        load.wait()
    perm = jnp.broadcast_to(perm_ref[...].astype(F32), (16, 64)).astype(BF16)
    pair = one_hot(iota(1)[:64] // 2 == iota(0)[:64])
    target = dot_nn(perm, pair)[:1] * 2.0 + (iota(1)[:1] % 2).astype(F32)
    placing = one_hot(iota(0).astype(F32) == target)
    for k in range(2, 4):
        entered(k)
    for a in range(8):
        activation(a)
    for k in range(4, 8):
        entered(k)
    recv_mg[:, slab(b), :] = swapped(tmp, b)

    @pl.when(at_edge)
    def _():
        for peer in [*plane, edge_peer]:
            signal(edge_sem, peer)

    for s in near:
        send_act[s] = swapped(act, s)
        act_copy(s, b).start()
    for s in far:
        send_act[s] = swapped(act, s)
    recv_act[:, slab(b), :] = swapped(act, b)

    @pl.when(jnp.logical_not(inner >= 3))
    def _():
        for s in far:
            act_copy(s, b).start()

    @pl.when(at_edge)
    def _():
        pl.semaphore_wait(edge_sem, 11)
        for k in range(1, 4):
            signal(edge_x_sem, x_peer(k))
        pl.semaphore_wait(edge_x_sem, 3)
        for k in range(1, 8):
            signal(open_sem, ((b + k) % 8, t))

    @pl.when(jnp.logical_not(at_edge))
    def _():
        pl.semaphore_wait(open_sem, 1)

    for s in others:
        mg_copy(s, s).wait_recv()

    @pl.when(inner >= 3)
    def _():
        for s in far:
            act_copy(s, b).start()

    sends = []

    def copy(send_sem, recv_sem, n, at_src, at_dst, src, dst, peer):
        return pltpu.make_async_remote_copy(
            src_ref=src,
            dst_ref=dst,
            send_sem=send_sem.at[n, at_src],
            recv_sem=recv_sem.at[n, at_dst],
            device_id=peer,
            device_id_type=MESH,
        )

    def q_sum(n, src, land):
        for k in (4, 5, 3, 2, 6, 7, 1):
            to = (q + k) % 8
            c = copy(rs_send, rs_recv, n, to, q, src(to), land(q), q_peer(k))
            c.start()
            sends.append(c)
        total = src(q)[...].astype(F32)
        for k in range(1, 8):
            at = (q + k) % 8
            copy(rs_send, rs_recv, n, at, at, src(at), land(at), q_peer(k)).wait_recv()
            total = total + land(at)[...].astype(F32)
        return total.astype(BF16)

    def last_copy(u, g, h, k, src):
        to = ring(x, k)
        return pltpu.make_async_remote_copy(
            src_ref=src.at[to],
            dst_ref=r_last.at[g, zh * 4 + x],
            send_sem=last_send.at[u, to],
            recv_sem=last_recv.at[g, zh * 4 + x],
            device_id=(b, h * 32 + to * 8 + q),
            device_id_type=MESH,
        )

    def last_start(h, pick):
        for k in range(4):
            goes = pick(ring(x, k))
            if k == 0:
                goes = jnp.logical_and(goes, zh != h)

            @pl.when(goes)
            def _():
                last_copy(0, 0, h, k, sq_late.at[0]).start()

        @pl.when(jnp.logical_and(pick(x), zh == h))
        def _():
            r_last[0, zh * 4 + x] = sq_late[0, x]

    def last_drain(*which):
        for k in range(1, 4):
            last_copy(*which[:3], k, which[3]).wait_send()

        @pl.when(zh != which[2])
        def _():
            last_copy(*which[:3], 0, which[3]).wait_send()

    def across(g, src):
        return pltpu.make_async_remote_copy(
            src_ref=src,
            dst_ref=r_across.at[g],
            send_sem=across_send.at[g],
            recv_sem=across_recv.at[g],
            device_id=zh_peer,
            device_id_type=MESH,
        )

    def early_copy(to, at, k):
        return pltpu.make_async_remote_copy(
            src_ref=sq_early.at[:, to],
            dst_ref=r_x.at[at],
            send_sem=x_send.at[to],
            recv_sem=x_recv.at[at],
            device_id=x_peer(k),
            device_id_type=MESH,
        )

    def put(total, out_ref):
        for a in range(NBL):
            out_ref[a] = total[2 * a : 2 * a + 2]

    def second(at, count, sources, store):
        for s in sources:
            act_copy(s, s).wait_recv()
        rows = pl.ds(pl.multiple_of(at * 16, 16), count * 16)
        for d in range(NBL):
            cols = slice(d * BS, (d + 1) * BS)
            part[d, : count * 16] = dot_nn(
                recv_act[d, rows, :], og_ref[:, cols]
            ).astype(BF16)
        for s in range(count):
            store[at % 4 + s] = swapped(part, s).reshape(8, 16, BS)

    for a in range(NBL):
        cols = slice(a * BS, (a + 1) * BS)
        pg = (recv_mg[a].astype(F32) * dgelu[a]).astype(BF16)
        tmp[a] = pg
        grad = dot_nn(pg, x_ref[:, cols]).astype(BF16)
        part[a] = dot_tn(grad, placing).astype(BF16)
    for s in range(NBL):
        g_early[s // 4, s % 4] = swapped(part, s).reshape(8, 16, BS)
    second(4 * half, 4, near, g_early.at[2])
    sq_early[...] = q_sum(0, lambda to: g_early.at[:, :, to], lambda at: rq_early.at[at])
    for k in range(1, 4):
        early_copy(ring(x, k), x, k).start()
    total = sq_early[:, x].astype(F32)
    for k in range(1, 4):
        at = ring(x, k)
        early_copy(at, at, k).wait_recv()
        total = total + r_x[at].astype(F32)
    s_x[...] = total.astype(BF16)
    across(0, s_x.at[1 - zh]).start()

    @pl.when(zh != half)
    def _():
        across(1, s_x.at[2]).start()

    for a in range(NBL):
        cols = slice(a * BS, (a + 1) * BS)
        ig_ref[:, cols] = dot_tn(tmp[a], wm[a]).astype(BF16)

    inmost = 3 * half
    outer = pl.ds(1 - half, 3)
    second(4 - 4 * half + 1 - half, 3, far[1:], g_late.at[0])
    sq_late[0, outer] = q_sum(
        1, lambda to: g_late.at[0, outer, to], lambda at: rq_late.at[at, 0, outer]
    )
    last_start(1 - half, lambda to: to != inmost)
    second(far[0], 1, far[:1], g_late.at[0])
    sq_late[0, inmost] = q_sum(
        2, lambda to: g_late.at[0, inmost, to], lambda at: rq_late.at[at, 0, inmost]
    )
    last_start(1 - half, lambda to: to == inmost)
    last = (0, 0, 1 - half, sq_late.at[0])

    across(0, s_x.at[1 - zh]).wait_recv()
    put(s_x[zh].astype(F32) + r_across[0].astype(F32), fg_ref)

    @pl.when(zh == half)
    def _():
        across(1, s_x.at[2]).wait_recv()
        put(s_x[2].astype(F32) + r_across[1].astype(F32), lg_ref)

    @pl.when(zh != half)
    def _():
        for k in range(1, 8):
            at = (zh * 4 + x + k) % 8
            pltpu.make_async_remote_copy(
                src_ref=r_last.at[0, at],
                dst_ref=r_last.at[0, at],
                send_sem=last_send.at[0, 0],
                recv_sem=last_recv.at[0, at],
                device_id=zh_peer,
                device_id_type=MESH,
            ).wait_recv()
        total = r_last[0, 0].astype(F32)
        for at in range(1, 8):
            total = total + r_last[0, at].astype(F32)
        put(total, lg_ref)

    for s in others:
        mg_copy(s, b).wait_send()
        act_copy(s, b).wait_send()
    for c in sends:
        c.wait_send()
    last_drain(*last)
    for k in range(1, 4):
        early_copy(ring(x, k), x, k).wait_send()
    across(0, s_x.at[1 - zh]).wait_send()

    @pl.when(zh != half)
    def _():
        across(1, s_x.at[2]).wait_send()


def publish(fg_in, lg_in, ig_in, fg_out, lg_out, ig_out, sem):
    copies = [
        pltpu.make_async_copy(src, dst, sem.at[i])
        for i, (src, dst) in enumerate(((ig_in, ig_out), (fg_in, fg_out), (lg_in, lg_out)))
    ]
    for copy in copies:
        copy.start()
    for copy in copies:
        copy.wait()


def per_device(tokens, first_blocks, latter_factor_blocks, block_perm, out_grad):
    vmem = pl.BlockSpec(memory_space=pltpu.VMEM)
    hbm = pl.BlockSpec(memory_space=pltpu.HBM)
    tokens, first_blocks, latter_factor_blocks, block_perm, out_grad = [pltpu.with_memory_space_constraint(v, pltpu.HBM) for v in (tokens, first_blocks, latter_factor_blocks, block_perm.reshape(1, 64), out_grad)]
    outs = pl.pallas_call(
        kernel,
        out_shape=(
            jax.ShapeDtypeStruct((NBL, 2, BS), F32),
            jax.ShapeDtypeStruct((NBL, 2, BS), F32),
            jax.ShapeDtypeStruct((ROWS, NBL * BS), BF16),
        ),
        in_specs=[hbm] * 5,
        out_specs=[vmem] * 3,
        scratch_shapes=[
            pltpu.VMEM((ROWS, NBL * BS), BF16),
            pltpu.VMEM((NBL, BS, BS), BF16),
            pltpu.VMEM((NBL, BS, BS), BF16),
            pltpu.VMEM((1, 64), jnp.int32),
            pltpu.VMEM((ROWS, NBL * BS), BF16),
            pltpu.SemaphoreType.DMA((5,)),
            pltpu.VMEM((NBL, BS, BS), BF16),
            pltpu.VMEM((NBL, BS, ROWS), BF16),
            pltpu.VMEM((NBL, BS, ROWS), BF16),
            pltpu.VMEM((NBL, BS, ROWS), F32),
            pltpu.VMEM((NBL, NBL, 16, ROWS), BF16),
            pltpu.VMEM((NBL, BS, ROWS), BF16),
            pltpu.VMEM((NBL, NBL, 16, ROWS), BF16),
            pltpu.VMEM((NBL, BS, ROWS), BF16),
            pltpu.VMEM((NBL, BS, BS), BF16),
            pltpu.VMEM((3, 4, 8, 16, BS), BF16),
            pltpu.VMEM((8, 3, 4, 16, BS), BF16),
            pltpu.VMEM((3, 4, 16, BS), BF16),
            pltpu.VMEM((1, 4, 8, 16, BS), BF16),
            pltpu.VMEM((8, 1, 4, 16, BS), BF16),
            pltpu.VMEM((1, 4, 16, BS), BF16),
            pltpu.VMEM((1, 8, 16, BS), BF16),
            pltpu.VMEM((4, 3, 16, BS), BF16),
            pltpu.VMEM((3, 16, BS), BF16),
            pltpu.VMEM((2, 16, BS), BF16),
            pltpu.SemaphoreType.DMA((2, NBL)),
            pltpu.SemaphoreType.DMA((2, NBL)),
            pltpu.SemaphoreType.DMA((3, 8)),
            pltpu.SemaphoreType.DMA((3, 8)),
            pltpu.SemaphoreType.DMA((1, 4)),
            pltpu.SemaphoreType.DMA((1, 8)),
            pltpu.SemaphoreType.DMA((4,)),
            pltpu.SemaphoreType.DMA((4,)),
            pltpu.SemaphoreType.DMA((2,)),
            pltpu.SemaphoreType.DMA((2,)),
            pltpu.SemaphoreType.REGULAR,
            pltpu.SemaphoreType.REGULAR,
            pltpu.SemaphoreType.REGULAR,
            pltpu.SemaphoreType.REGULAR((8,)),
            pltpu.SemaphoreType.REGULAR((8,)),
        ],
        compiler_params=pltpu.CompilerParams(
            collective_id=0, has_side_effects=True, vmem_limit_bytes=24 * 2**20
        ),
    )(tokens, first_blocks, latter_factor_blocks, block_perm, out_grad)
    return pl.pallas_call(
        publish,
        out_shape=tuple(jax.ShapeDtypeStruct(o.shape, o.dtype) for o in outs),
        in_specs=[vmem] * 3,
        out_specs=[hbm] * 3,
        scratch_shapes=[pltpu.SemaphoreType.DMA((3,))],
        compiler_params=pltpu.CompilerParams(vmem_limit_bytes=16 * 2**20),
    )(*outs)


def solution(mesh):
    return jax.shard_map(
        per_device,
        mesh=mesh,
        in_specs=(
            P("tok", "blk"),
            P("blk", None, None),
            P("blk", None, None),
            P(),
            P("tok", "blk"),
        ),
        out_specs=(P("blk", "tok", None), P("blk", "tok", None), P("tok", "blk")),
        check_vma=False,
    )
```

```python
import jax
import jax.numpy as jnp
from jax import lax
from jax.experimental import pallas as pl
from jax.experimental.pallas import tpu as pltpu
from jax.sharding import PartitionSpec as P

MESH = pl.DeviceIdType.MESH
F32 = jnp.float32
BF16 = jnp.bfloat16
ROWS = 256
BS = 128
NBL = 8


def dot_nn(a, b):
    return lax.dot_general(a, b, (((1,), (0,)), ((), ())), preferred_element_type=F32)


def dot_nt(a, b):
    return lax.dot_general(a, b, (((1,), (1,)), ((), ())), preferred_element_type=F32)


def dot_tn(a, b):
    return lax.dot_general(a, b, (((0,), (0,)), ((), ())), preferred_element_type=F32)


def iota(dim):
    return lax.broadcasted_iota(jnp.int32, (BS, BS), dim)


def one_hot(hit):
    return jnp.where(hit, 1.0, 0.0).astype(BF16)


def kernel(
    x_hbm, w_hbm, l_hbm, perm_hbm, og_hbm,
    fg_ref, lg_ref, ig_ref,
    x_ref, w_ref, l_ref, perm_ref, og_ref, in_sem,
    wm, tmp, act, dgelu, send_mg, recv_mg, send_act, recv_act, part,
    g_early, rq_early, sq_early, g_late, rq_late, sq_late, r_last, r_x, s_x, r_across,
    a2a_send, a2a_recv, rs_send, rs_recv, last_send, last_recv, x_send, x_recv, across_send, across_recv, edge_sem, edge_x_sem, open_sem, up_sem, down_sem,
):
    b = lax.axis_index("blk")
    t = lax.axis_index("tok")
    zh, x, q = t // 32, (t // 8) % 4, t % 8
    half, place = b // 4, b % 4

    def ring(at, k):
        return (at + k) % 4

    zh_peer = (b, t + 32 - 64 * zh)

    def q_peer(k):
        return (b, t + (q + k) % 8 - q)

    def x_peer(k):
        return (b, t + (ring(x, k) - x) * 8)

    far = [half * (3 - k) + (1 - half) * (4 + k) for k in range(4)]
    near = [half * 4 + ring(place, k) for k in range(1, 4)]
    others = far + near
    inner = half * place + (1 - half) * (3 - place)

    at_edge = b == 7 - 7 * zh
    edge_peer = (7 - b, t + 32 - 64 * zh)

    def signal(sem, peer):
        pl.semaphore_signal(sem, inc=1, device_id=peer, device_id_type=MESH)

    barrier = pltpu.get_barrier_semaphore()
    plane = [q_peer(k) for k in range(1, 8)] + [x_peer(k) for k in range(1, 4)]

    @pl.when(b > 0)
    def _():
        signal(barrier, (b - 1, t))

    @pl.when(b < 7)
    def _():
        signal(barrier, (b + 1, t))

    @pl.when(at_edge)
    def _():
        for peer in [*plane, edge_peer]:
            signal(barrier, peer)

    loads = [
        pltpu.make_async_copy(src, dst, in_sem.at[i])
        for i, (src, dst) in enumerate(
            (
                (og_hbm, og_ref),
                (l_hbm, l_ref),
                (w_hbm, w_ref),
                (x_hbm, x_ref),
                (perm_hbm, perm_ref),
            )
        )
    ]
    for load in loads:
        load.start()

    row, col = iota(0), iota(1)
    swap = one_hot(col == ((row >> 1) & 7) * 16 + (row >> 4) * 2 + (row & 1))

    def slab(s):
        return pl.ds(pl.multiple_of(s * 16, 16), 16)

    def a2a(phase, to, at, send, recv):
        return pltpu.make_async_remote_copy(
            src_ref=send.at[to],
            dst_ref=recv.at[:, slab(at), :],
            send_sem=a2a_send.at[phase, to],
            recv_sem=a2a_recv.at[phase, at],
            device_id=(to, t),
            device_id_type=MESH,
        )

    def mg_copy(to, at):
        return a2a(0, to, at, send_mg, recv_mg)

    def act_copy(to, at):
        return a2a(1, to, at, send_act, recv_act)

    def swapped(src, s):
        width = src.shape[-1]
        chunk = src[:, slab(s), :].reshape(BS, width)
        return dot_nn(swap, chunk).astype(BF16).reshape(NBL, 16, width)

    loads[0].wait()
    loads[1].wait()
    for d in range(NBL):
        cols = slice(d * BS, (d + 1) * BS)
        tmp[d] = dot_nt(l_ref[d], og_ref[:, cols]).astype(BF16)

    def entered(k):
        up, down = b + k, b - k

        @pl.when(down >= 0)
        def _():
            if k > 1:
                pl.semaphore_wait(down_sem.at[k], 1)
            if k < 7:

                @pl.when(b < 7)
                def _():
                    signal(down_sem.at[k + 1], (b + 1, t))

            send_mg[down] = swapped(tmp, down)
            mg_copy(down, b).start()

        @pl.when(up < 8)
        def _():
            if k > 1:
                pl.semaphore_wait(up_sem.at[k], 1)
            if k < 7:

                @pl.when(b > 0)
                def _():
                    signal(up_sem.at[k + 1], (b - 1, t))

            send_mg[up] = swapped(tmp, up)
            mg_copy(up, b).start()

    def activation(a):
        cols = slice(a * BS, (a + 1) * BS)
        wm[a] = dot_nt(placing, w_ref[a]).astype(BF16)
        pre = dot_nt(wm[a], x_ref[:, cols])
        cdf = 0.5 * (1.0 + lax.erf(pre * 0.7071067811865476))
        act[a] = (pre * cdf).astype(BF16)
        dgelu[a] = cdf + pre * 0.3989422804014327 * jnp.exp(-0.5 * pre * pre)

    pl.semaphore_wait(
        barrier,
        jnp.where(b > 0, 1, 0) + jnp.where(b < 7, 1, 0) + jnp.where(at_edge, 11, 0),
    )
    entered(1)
    for load in loads[2:]:
        load.wait()
    perm = jnp.broadcast_to(perm_ref[...].astype(F32), (16, 64)).astype(BF16)
    pair = one_hot(iota(1)[:64] // 2 == iota(0)[:64])
    target = dot_nn(perm, pair)[:1] * 2.0 + (iota(1)[:1] % 2).astype(F32)
    placing = one_hot(iota(0).astype(F32) == target)
    for k in range(2, 6):
        activation(2 * k - 4)
        activation(2 * k - 3)
        entered(k)
    entered(6)
    entered(7)
    recv_mg[:, slab(b), :] = swapped(tmp, b)

    @pl.when(at_edge)
    def _():
        for peer in [*plane, edge_peer]:
            signal(edge_sem, peer)

    for s in near:
        send_act[s] = swapped(act, s)
        act_copy(s, b).start()
    for s in far:
        send_act[s] = swapped(act, s)
    recv_act[:, slab(b), :] = swapped(act, b)

    @pl.when(jnp.logical_not(inner >= 3))
    def _():
        for s in far:
            act_copy(s, b).start()

    @pl.when(at_edge)
    def _():
        pl.semaphore_wait(edge_sem, 11)
        for k in range(1, 4):
            signal(edge_x_sem, x_peer(k))
        pl.semaphore_wait(edge_x_sem, 3)
        for k in range(1, 8):
            signal(open_sem, ((b + k) % 8, t))

    @pl.when(jnp.logical_not(at_edge))
    def _():
        pl.semaphore_wait(open_sem, 1)

    for s in others:
        mg_copy(s, s).wait_recv()

    @pl.when(inner >= 3)
    def _():
        for s in far:
            act_copy(s, b).start()

    sends = []

    def copy(send_sem, recv_sem, n, at_src, at_dst, src, dst, peer):
        return pltpu.make_async_remote_copy(
            src_ref=src,
            dst_ref=dst,
            send_sem=send_sem.at[n, at_src],
            recv_sem=recv_sem.at[n, at_dst],
            device_id=peer,
            device_id_type=MESH,
        )

    def q_sum(n, src, land):
        for k in (4, 5, 3, 2, 6, 7, 1):
            to = (q + k) % 8
            c = copy(rs_send, rs_recv, n, to, q, src(to), land(q), q_peer(k))
            c.start()
            sends.append(c)
        total = src(q)[...].astype(F32)
        for k in range(1, 8):
            at = (q + k) % 8
            copy(rs_send, rs_recv, n, at, at, src(at), land(at), q_peer(k)).wait_recv()
            total = total + land(at)[...].astype(F32)
        return total.astype(BF16)

    def last_copy(u, g, h, k, src):
        to = ring(x, k)
        return pltpu.make_async_remote_copy(
            src_ref=src.at[to],
            dst_ref=r_last.at[g, zh * 4 + x],
            send_sem=last_send.at[u, to],
            recv_sem=last_recv.at[g, zh * 4 + x],
            device_id=(b, h * 32 + to * 8 + q),
            device_id_type=MESH,
        )

    def last_start(h, pick):
        for k in range(4):
            goes = pick(ring(x, k))
            if k == 0:
                goes = jnp.logical_and(goes, zh != h)

            @pl.when(goes)
            def _():
                last_copy(0, 0, h, k, sq_late.at[0]).start()

        @pl.when(jnp.logical_and(pick(x), zh == h))
        def _():
            r_last[0, zh * 4 + x] = sq_late[0, x]

    def last_drain(*which):
        for k in range(1, 4):
            last_copy(*which[:3], k, which[3]).wait_send()

        @pl.when(zh != which[2])
        def _():
            last_copy(*which[:3], 0, which[3]).wait_send()

    def across(g, src):
        return pltpu.make_async_remote_copy(
            src_ref=src,
            dst_ref=r_across.at[g],
            send_sem=across_send.at[g],
            recv_sem=across_recv.at[g],
            device_id=zh_peer,
            device_id_type=MESH,
        )

    def early_copy(to, at, k):
        return pltpu.make_async_remote_copy(
            src_ref=sq_early.at[:, to],
            dst_ref=r_x.at[at],
            send_sem=x_send.at[to],
            recv_sem=x_recv.at[at],
            device_id=x_peer(k),
            device_id_type=MESH,
        )

    def put(total, out_ref):
        for a in range(NBL):
            out_ref[a] = total[2 * a : 2 * a + 2]

    def second(at, count, sources, store):
        for s in sources:
            act_copy(s, s).wait_recv()
        rows = pl.ds(pl.multiple_of(at * 16, 16), count * 16)
        for d in range(NBL):
            cols = slice(d * BS, (d + 1) * BS)
            part[d, : count * 16] = dot_nn(
                recv_act[d, rows, :], og_ref[:, cols]
            ).astype(BF16)
        for s in range(count):
            store[at % 4 + s] = swapped(part, s).reshape(8, 16, BS)

    for a in range(NBL):
        cols = slice(a * BS, (a + 1) * BS)
        pg = (recv_mg[a].astype(F32) * dgelu[a]).astype(BF16)
        tmp[a] = pg
        grad = dot_nn(pg, x_ref[:, cols]).astype(BF16)
        part[a] = dot_tn(grad, placing).astype(BF16)
    for s in range(NBL):
        g_early[s // 4, s % 4] = swapped(part, s).reshape(8, 16, BS)
    second(4 * half, 4, near, g_early.at[2])
    sq_early[...] = q_sum(0, lambda to: g_early.at[:, :, to], lambda at: rq_early.at[at])
    for k in range(1, 4):
        early_copy(ring(x, k), x, k).start()
    total = sq_early[:, x].astype(F32)
    for k in range(1, 4):
        at = ring(x, k)
        early_copy(at, at, k).wait_recv()
        total = total + r_x[at].astype(F32)
    s_x[...] = total.astype(BF16)
    across(0, s_x.at[1 - zh]).start()

    @pl.when(zh != half)
    def _():
        across(1, s_x.at[2]).start()

    for a in range(NBL):
        cols = slice(a * BS, (a + 1) * BS)
        ig_ref[:, cols] = dot_tn(tmp[a], wm[a]).astype(BF16)

    inmost = 3 * half
    outer = pl.ds(1 - half, 3)
    second(4 - 4 * half + 1 - half, 3, far[1:], g_late.at[0])
    sq_late[0, outer] = q_sum(
        1, lambda to: g_late.at[0, outer, to], lambda at: rq_late.at[at, 0, outer]
    )
    last_start(1 - half, lambda to: to != inmost)
    second(far[0], 1, far[:1], g_late.at[0])
    sq_late[0, inmost] = q_sum(
        2, lambda to: g_late.at[0, inmost, to], lambda at: rq_late.at[at, 0, inmost]
    )
    last_start(1 - half, lambda to: to == inmost)
    last = (0, 0, 1 - half, sq_late.at[0])

    across(0, s_x.at[1 - zh]).wait_recv()
    put(s_x[zh].astype(F32) + r_across[0].astype(F32), fg_ref)

    @pl.when(zh == half)
    def _():
        across(1, s_x.at[2]).wait_recv()
        put(s_x[2].astype(F32) + r_across[1].astype(F32), lg_ref)

    @pl.when(zh != half)
    def _():
        for k in range(1, 8):
            at = (zh * 4 + x + k) % 8
            pltpu.make_async_remote_copy(
                src_ref=r_last.at[0, at],
                dst_ref=r_last.at[0, at],
                send_sem=last_send.at[0, 0],
                recv_sem=last_recv.at[0, at],
                device_id=zh_peer,
                device_id_type=MESH,
            ).wait_recv()
        total = r_last[0, 0].astype(F32)
        for at in range(1, 8):
            total = total + r_last[0, at].astype(F32)
        put(total, lg_ref)

    for s in others:
        mg_copy(s, b).wait_send()
        act_copy(s, b).wait_send()
    for c in sends:
        c.wait_send()
    last_drain(*last)
    for k in range(1, 4):
        early_copy(ring(x, k), x, k).wait_send()
    across(0, s_x.at[1 - zh]).wait_send()

    @pl.when(zh != half)
    def _():
        across(1, s_x.at[2]).wait_send()


def publish(fg_in, lg_in, ig_in, fg_out, lg_out, ig_out, sem):
    copies = [
        pltpu.make_async_copy(src, dst, sem.at[i])
        for i, (src, dst) in enumerate(((ig_in, ig_out), (fg_in, fg_out), (lg_in, lg_out)))
    ]
    for copy in copies:
        copy.start()
    for copy in copies:
        copy.wait()


def per_device(tokens, first_blocks, latter_factor_blocks, block_perm, out_grad):
    vmem = pl.BlockSpec(memory_space=pltpu.VMEM)
    hbm = pl.BlockSpec(memory_space=pltpu.HBM)
    tokens, first_blocks, latter_factor_blocks, block_perm, out_grad = [pltpu.with_memory_space_constraint(v, pltpu.HBM) for v in (tokens, first_blocks, latter_factor_blocks, block_perm.reshape(1, 64), out_grad)]
    outs = pl.pallas_call(
        kernel,
        out_shape=(
            jax.ShapeDtypeStruct((NBL, 2, BS), F32),
            jax.ShapeDtypeStruct((NBL, 2, BS), F32),
            jax.ShapeDtypeStruct((ROWS, NBL * BS), BF16),
        ),
        in_specs=[hbm] * 5,
        out_specs=[vmem] * 3,
        scratch_shapes=[
            pltpu.VMEM((ROWS, NBL * BS), BF16),
            pltpu.VMEM((NBL, BS, BS), BF16),
            pltpu.VMEM((NBL, BS, BS), BF16),
            pltpu.VMEM((1, 64), jnp.int32),
            pltpu.VMEM((ROWS, NBL * BS), BF16),
            pltpu.SemaphoreType.DMA((5,)),
            pltpu.VMEM((NBL, BS, BS), BF16),
            pltpu.VMEM((NBL, BS, ROWS), BF16),
            pltpu.VMEM((NBL, BS, ROWS), BF16),
            pltpu.VMEM((NBL, BS, ROWS), F32),
            pltpu.VMEM((NBL, NBL, 16, ROWS), BF16),
            pltpu.VMEM((NBL, BS, ROWS), BF16),
            pltpu.VMEM((NBL, NBL, 16, ROWS), BF16),
            pltpu.VMEM((NBL, BS, ROWS), BF16),
            pltpu.VMEM((NBL, BS, BS), BF16),
            pltpu.VMEM((3, 4, 8, 16, BS), BF16),
            pltpu.VMEM((8, 3, 4, 16, BS), BF16),
            pltpu.VMEM((3, 4, 16, BS), BF16),
            pltpu.VMEM((1, 4, 8, 16, BS), BF16),
            pltpu.VMEM((8, 1, 4, 16, BS), BF16),
            pltpu.VMEM((1, 4, 16, BS), BF16),
            pltpu.VMEM((1, 8, 16, BS), BF16),
            pltpu.VMEM((4, 3, 16, BS), BF16),
            pltpu.VMEM((3, 16, BS), BF16),
            pltpu.VMEM((2, 16, BS), BF16),
            pltpu.SemaphoreType.DMA((2, NBL)),
            pltpu.SemaphoreType.DMA((2, NBL)),
            pltpu.SemaphoreType.DMA((3, 8)),
            pltpu.SemaphoreType.DMA((3, 8)),
            pltpu.SemaphoreType.DMA((1, 4)),
            pltpu.SemaphoreType.DMA((1, 8)),
            pltpu.SemaphoreType.DMA((4,)),
            pltpu.SemaphoreType.DMA((4,)),
            pltpu.SemaphoreType.DMA((2,)),
            pltpu.SemaphoreType.DMA((2,)),
            pltpu.SemaphoreType.REGULAR,
            pltpu.SemaphoreType.REGULAR,
            pltpu.SemaphoreType.REGULAR,
            pltpu.SemaphoreType.REGULAR((8,)),
            pltpu.SemaphoreType.REGULAR((8,)),
        ],
        compiler_params=pltpu.CompilerParams(
            collective_id=0, has_side_effects=True, vmem_limit_bytes=24 * 2**20
        ),
    )(tokens, first_blocks, latter_factor_blocks, block_perm, out_grad)
    return pl.pallas_call(
        publish,
        out_shape=tuple(jax.ShapeDtypeStruct(o.shape, o.dtype) for o in outs),
        in_specs=[vmem] * 3,
        out_specs=[hbm] * 3,
        scratch_shapes=[pltpu.SemaphoreType.DMA((3,))],
        compiler_params=pltpu.CompilerParams(vmem_limit_bytes=16 * 2**20),
    )(*outs)


def solution(mesh):
    return jax.shard_map(
        per_device,
        mesh=mesh,
        in_specs=(
            P("tok", "blk"),
            P("blk", None, None),
            P("blk", None, None),
            P(),
            P("tok", "blk"),
        ),
        out_specs=(P("blk", "tok", None), P("blk", "tok", None), P("tok", "blk")),
        check_vma=False,
    )
```
